32 devices in a mesh: gx: 4 (over z), gy: 8 (over y, x, core).
Axes of the slice: x: 2, y: 2, z: 4, core: 2. Of those that a mesh axis runs over, the one named last changes fastest.
Arguments:
- blocks: float32 [192, 128, 4096], P(('gx', 'gy')), may hold values from -0.046875 to 0.046875
- features: float32 [512, 128, 512], P(('gx', 'gy')), may hold values from -6 to 6
- col_ids: int32 [192, 32], P(('gx', 'gy')), may hold values from 0 to 15
- row_ids: int32 [192], P(('gx', 'gy')), may hold values from 0 to 31
- factor: float32 [512, 512], replicated, may hold values from -0.25 to 0.25
Outputs:
- owned_rows: float32 [4096, 512], P(('gx', 'gy'))
- returned: float32 [24576, 512], P(('gx', 'gy'))
The draws below stay inside these ranges and needn't reach their ends.
Inputs may be any that keep to these rules, and one draw needn't show every extreme that they name: `row_ids`: row block r is owned by device r, counted over gx+gy with gx slowest. Row blocks are named with a power-law skew; one device may name a row block more than once. `col_ids`: indices into the device's own feature tiles.
All inputs are finite; a program needn't handle non-finite values.
Results may differ from the reference program's by a relative error of at most 0.00013.
Values sent between devices are 32-bit elements; how exact they have to be, the bound alone decides.
No kernel may reach another device: no remote copies, remote signals or barrier semaphores. Data moves between devices by JAX's collectives and lax.ppermute only.
A program may use at most 192 MiB of HBM per device.

```python
import math
import jax
import jax.numpy as jnp
import numpy as np
from jax import lax

B = 128
FEAT = 512
SLOTS = 6
BPR = 32
FT = 16
ROWBLOCKS = 32
DEVICES = 32


def with_ends(array, own_key, smallest, largest):
    index_at = [jax.random.randint(jax.random.fold_in(own_key, axis), (), 0, length) for axis, length in enumerate(array.shape)]
    main_axis = array.shape.index(max(array.shape))
    beside = index_at[:main_axis] + [(index_at[main_axis] + 1) % array.shape[main_axis]] + index_at[main_axis + 1:]
    return array.at[tuple(index_at)].set(smallest).at[tuple(beside)].set(largest)


def block_scale(stream_key, shape, pieces, low, top_value):
    loudness, own = 1.0, jax.random.fold_in(stream_key, 6)
    for axis_at, shards_of in pieces:
        draws = jnp.exp(jax.random.uniform(jax.random.fold_in(own, axis_at), (shards_of,), jnp.float32, low / len(pieces), top_value / len(pieces)))
        loudness = loudness * jnp.repeat(draws, shape[axis_at] // shards_of).reshape([-1 if axis == axis_at else 1 for axis in range(len(shape))])
    return loudness


def rank_table(number_of, slope):
    portions = [(1 << 20) // math.isqrt(grade ** slope) + 1 for grade in range(1, number_of + 1)]
    spread = 1 + sum(portions) // (1 << 30)
    return np.cumsum(np.array([max(1, weight // spread) for weight in portions]))


def skewed_ids(own_key, extent, amount, slope):
    table = rank_table(amount, slope)
    ticket = jax.random.randint(jax.random.fold_in(own_key, 1), extent, 0, int(table[amount - 1]))
    standing = jnp.searchsorted(jnp.asarray(table, jnp.int32), ticket, side="right")
    return jax.random.permutation(jax.random.fold_in(own_key, 2), amount)[standing].astype(jnp.int32)


def gaussian(rng, extent, spread, reach, shards=(), kind=jnp.bfloat16):
    drawn = jax.random.normal(rng, extent, jnp.float32) * spread
    if len(shards) > 0:
        drawn = block_scale(rng, extent, shards, -0.22, 0.18) * drawn
    return jnp.clip(drawn, min=-reach, max=reach).astype(kind)


def setup_inputs(seed: int = 0) -> dict:
    key_list = jax.random.split(jax.random.key(seed), 6)
    blocks = gaussian(key_list[0], (DEVICES * SLOTS, B, BPR * B), (4 * BPR * B) ** -0.5, 0.046875, ((0, 32),), jnp.float32)
    features = gaussian(key_list[1], (DEVICES * FT, B, FEAT), 1.0, 6.0, ((0, 32),), jnp.float32)
    col_ids = with_ends(jax.random.randint(key_list[2], (DEVICES * SLOTS, BPR), 0, FT), jax.random.fold_in(key_list[2], 1), 0, FT - 1).astype(jnp.int32)
    row_ids = with_ends(skewed_ids(key_list[3], (DEVICES * SLOTS,), ROWBLOCKS, 2), jax.random.fold_in(key_list[3], 3), 0, ROWBLOCKS - 1).astype(jnp.int32)
    factor = gaussian(key_list[4], (FEAT, FEAT), FEAT ** -0.5, 0.25, (), jnp.float32)
    return dict(blocks=blocks, features=features, col_ids=col_ids, row_ids=row_ids, factor=factor)


HIGHEST = lax.Precision.HIGHEST


def reference(blocks, features, col_ids, row_ids, factor):
    dev_count = blocks.shape[0] // SLOTS
    blk_all = blocks.reshape(dev_count, SLOTS, B, BPR * B)
    feat_all = features.reshape(dev_count, FT, B, FEAT)
    col_all = col_ids.reshape(dev_count, SLOTS, BPR)

    def device_rows(packed):
        blk_rows, feat_rows, col_rows = packed
        gathered = feat_rows[col_rows].reshape(SLOTS, BPR * B, FEAT)
        return jnp.einsum("sik,skf->sif", blk_rows, gathered, precision=HIGHEST)

    partial_value = lax.map(device_rows, (blk_all, feat_all, col_all)).reshape(dev_count * SLOTS, B, FEAT)
    row_sums = jax.ops.segment_sum(partial_value, row_ids, num_segments=ROWBLOCKS)
    owned_rows = jnp.dot(jnp.tanh(row_sums).reshape(ROWBLOCKS * B, FEAT), factor,
                         precision=HIGHEST, preferred_element_type=jnp.float32)
    returned = owned_rows.reshape(ROWBLOCKS, B, FEAT)[row_ids].reshape(dev_count * SLOTS * B, FEAT)
    return owned_rows, returned
```

```python
import functools

import jax
import jax.numpy as jnp
from jax import lax
from jax.experimental import pallas as pl
from jax.experimental.pallas import tpu as pltpu
from jax.sharding import Mesh
from jax.sharding import PartitionSpec as P

F32 = jnp.float32
BF16 = jnp.bfloat16
VMEM_BYTES = 48 << 20


def split(value):
    high = value.astype(BF16)
    return high, (value - high.astype(F32)).astype(BF16)


def dot3(a_high, a_low, b_high, b_low):
    dot = functools.partial(jnp.dot, preferred_element_type=F32)
    return dot(a_high, b_high) + dot(a_high, b_low) + dot(a_low, b_high)


def product_kernel(
    group, peers, cols_ref, blocks_ref, features_ref, out_ref, total, a_high, a_low, f_high, f_low
):
    slot = pl.program_id(0)
    tiles, rows, feat = features_ref.shape
    per_row = cols_ref.shape[1]

    @pl.when(slot == 0)
    def _():
        def split_tile(tile, carry):
            high, low = split(features_ref[tile])
            at = pl.ds(pl.multiple_of(tile * rows, rows), rows)
            f_high[at, :] = high
            f_low[at, :] = low
            return carry

        lax.fori_loop(0, tiles, split_tile, 0)

    total[...] = jnp.zeros_like(total)
    for j in range(per_row):
        tile = cols_ref[slot, j]
        total[tile] = total[tile] + blocks_ref[0, :, j * rows : (j + 1) * rows]
    at = pl.ds(pl.multiple_of(lax.rem(slot, group) * rows, rows), rows)
    for tile in range(tiles):
        high, low = split(total[tile])
        a_high[at, tile * rows : (tile + 1) * rows] = high
        a_low[at, tile * rows : (tile + 1) * rows] = low

    @pl.when(lax.rem(slot, group) == group - 1)
    def _():
        width = min(feat, 256)
        for n in range(feat // width):
            cut = slice(n * width, (n + 1) * width)
            part = dot3(a_high[...], a_low[...], f_high[:, cut], f_low[:, cut])
            for g in range(group):
                out_ref[:, g, :, cut] = part[g * rows : (g + 1) * rows].reshape(
                    peers, rows // peers, width
                )


def product(blocks, features, col_ids, peers):
    slots, rows, width = blocks.shape
    tiles, _, feat = features.shape
    group = 2 if slots % 2 == 0 else 1
    return pl.pallas_call(
        functools.partial(product_kernel, group, peers),
        grid_spec=pltpu.PrefetchScalarGridSpec(
            num_scalar_prefetch=1,
            grid=(slots,),
            in_specs=[
                pl.BlockSpec((1, rows, width), lambda k, c: (k, 0, 0)),
                pl.BlockSpec(
                    (tiles, rows, feat), lambda k, c: (0, 0, 0), pipeline_mode=pl.Buffered(1)
                ),
            ],
            out_specs=pl.BlockSpec(
                (peers, group, rows // peers, feat), lambda k, c: (0, k // group, 0, 0)
            ),
            scratch_shapes=[
                pltpu.VMEM((tiles, rows, rows), F32),
                pltpu.VMEM((group * rows, tiles * rows), BF16),
                pltpu.VMEM((group * rows, tiles * rows), BF16),
                pltpu.VMEM((tiles * rows, feat), BF16),
                pltpu.VMEM((tiles * rows, feat), BF16),
            ],
        ),
        out_shape=jax.ShapeDtypeStruct((peers, slots, rows // peers, feat), F32),
        compiler_params=pltpu.CompilerParams(vmem_limit_bytes=VMEM_BYTES),
        name="product",
    )(col_ids, blocks, features)


def gather_sum_kernel(rows_ref, half_ref, pieces_ref, stay_ref, send_ref):
    peers, slots = pieces_ref.shape[:2]
    half_rows = stay_ref.shape[0]
    stay_ref[...] = jnp.zeros_like(stay_ref)
    send_ref[...] = jnp.zeros_like(send_ref)
    base = half_ref[0] * half_rows

    def add_peer(peer, carry):
        for slot in range(slots):
            row = rows_ref[peer * slots + slot] - base
            here = (row >= 0) & (row < half_rows)
            row = lax.select(row < 0, row + half_rows, row)
            row = lax.select(row >= half_rows, row - half_rows, row)

            @pl.when(here)
            def _():
                stay_ref[row] = stay_ref[row] + pieces_ref[peer, slot]

            @pl.when(jnp.logical_not(here))
            def _():
                send_ref[row] = send_ref[row] + pieces_ref[peer, slot]

        return carry

    lax.fori_loop(0, peers, add_peer, 0)


def gather_sum(group_rows, half, pieces, row_blocks):
    _, _, rows, feat = pieces.shape
    shape = jax.ShapeDtypeStruct((row_blocks // 2, rows, feat), F32)
    smem = pl.BlockSpec(memory_space=pltpu.SMEM)
    vmem = pl.BlockSpec(memory_space=pltpu.VMEM)
    return pl.pallas_call(
        gather_sum_kernel,
        in_specs=[smem, smem, vmem],
        out_specs=(vmem, vmem),
        out_shape=(shape, shape),
        compiler_params=pltpu.CompilerParams(vmem_limit_bytes=VMEM_BYTES),
        name="gather_sum",
    )(group_rows, half, pieces)


def update_kernel(mine_ref, theirs_ref, factor_ref, out_ref):
    count, rows, feat = out_ref.shape
    sums = jnp.tanh(mine_ref[...] + theirs_ref[...]).reshape(count * rows, feat)
    out = dot3(*split(sums), *split(factor_ref[...]))
    out_ref[...] = out.reshape(out_ref.shape)


def update(mine, theirs, factor):
    return pl.pallas_call(
        update_kernel,
        out_shape=jax.ShapeDtypeStruct(mine.shape, F32),
        compiler_params=pltpu.CompilerParams(vmem_limit_bytes=VMEM_BYTES),
        name="update",
    )(mine, theirs, factor)


def answer_kernel(rows_ref, half_ref, mine_ref, theirs_ref, out_ref):
    peers, places = out_ref.shape[:2]
    slots = places - 1
    half_rows = mine_ref.shape[0]
    base = half_ref[0] * half_rows

    def pick(peer, carry):
        for slot in range(slots):
            row = rows_ref[peer * slots + slot] - base
            here = (row >= 0) & (row < half_rows)
            row = lax.select(row < 0, row + half_rows, row)
            row = lax.select(row >= half_rows, row - half_rows, row)

            @pl.when(here)
            def _():
                out_ref[peer, slot] = mine_ref[row]

            @pl.when(jnp.logical_not(here))
            def _():
                out_ref[peer, slot] = theirs_ref[row]

        out_ref[peer, slots] = mine_ref[peer]
        return carry

    lax.fori_loop(0, peers, pick, 0)


def answer(group_rows, half, mine, theirs, peers, slots):
    _, rows, feat = mine.shape
    smem = pl.BlockSpec(memory_space=pltpu.SMEM)
    vmem = pl.BlockSpec(memory_space=pltpu.VMEM)
    return pl.pallas_call(
        answer_kernel,
        in_specs=[smem, smem, vmem, vmem],
        out_specs=vmem,
        out_shape=jax.ShapeDtypeStruct((peers, slots + 1, rows, feat), F32),
        compiler_params=pltpu.CompilerParams(vmem_limit_bytes=VMEM_BYTES),
        name="answer",
    )(group_rows, half, mine, theirs)


def local(axes, blocks, features, col_ids, row_ids, factor):
    half_axis, peer_axes = axes[0], axes[1:]
    slots, rows, _ = blocks.shape
    feat = features.shape[2]
    peers = lax.axis_size(peer_axes)
    halves = lax.axis_size(half_axis)
    row_blocks = peers * halves
    half = lax.axis_index(half_axis).astype(jnp.int32).reshape(1)
    group_rows = lax.all_gather(row_ids, peer_axes, tiled=True)

    pieces = product(blocks, features, col_ids, peers)
    pieces = lax.all_to_all(pieces, peer_axes, 0, 0)
    stay, send = gather_sum(group_rows, half, pieces, row_blocks)
    swap = [(0, 1), (1, 0)]
    got = lax.ppermute(send, half_axis, swap)
    mine = update(stay, got, factor)
    theirs = lax.ppermute(mine, half_axis, swap)
    answers = answer(group_rows, half, mine, theirs, peers, slots)
    answers = lax.all_to_all(answers, peer_axes, 0, 0)
    returned = answers[:, :slots].transpose(1, 0, 2, 3).reshape(slots * rows, feat)
    owned_rows = answers[:, slots].reshape(rows, feat)
    return owned_rows, returned


def solution(mesh):
    outer, inner = mesh.devices.shape
    devices = mesh.devices.reshape(2, outer // 2, inner)
    axes = ("half", "gx_low", "gy")
    split_mesh = Mesh(devices, axes)
    return jax.shard_map(
        functools.partial(local, axes),
        mesh=split_mesh,
        in_specs=(P(axes, None, None), P(axes, None, None), P(axes, None), P(axes), P()),
        out_specs=(P(axes, None), P(axes, None)),
        check_vma=False,
    )
```

```python
import functools

import jax
import jax.numpy as jnp
from jax import lax
from jax.experimental import pallas as pl
from jax.experimental.pallas import tpu as pltpu
from jax.sharding import Mesh
from jax.sharding import PartitionSpec as P

F32 = jnp.float32
BF16 = jnp.bfloat16
I32 = jnp.int32
LANES = 128
VMEM_BYTES = 40 << 20


def split(value):
    high = value.astype(BF16)
    return high, (value - high.astype(F32)).astype(BF16)


def dot3(a_high, a_low, b_high, b_low):
    dot = functools.partial(jnp.dot, preferred_element_type=F32)
    return dot(a_high, b_high) + dot(a_high, b_low) + dot(a_low, b_high)


def spec(space):
    return pl.BlockSpec(memory_space=space)


def params():
    return pltpu.CompilerParams(vmem_limit_bytes=VMEM_BYTES)


def product_kernel(
    with_ids, part_ref, ids_ref, blocks_ref, cols_hbm, features_hbm, out_ref,
    total, a_high, a_low, f_high, f_low, features, cols, sems,
):
    slot = pl.program_id(0)
    slots, per_row = cols.shape
    tiles, depth, feat = features.shape
    rows = blocks_ref.shape[1]
    peers, _, piece_rows, _ = out_ref.shape
    features_copy = pltpu.make_async_copy(features_hbm, features, sems.at[0])

    @pl.when(slot == 0)
    def _():
        cols_copy = pltpu.make_async_copy(cols_hbm, cols, sems.at[1])
        cols_copy.start()
        features_copy.start()
        cols_copy.wait()

    total[...] = jnp.zeros_like(total)
    for j in range(per_row):
        tile = cols[slot, j]
        total[tile] = total[tile] + blocks_ref[0, :, j * depth : (j + 1) * depth]
    at = pl.ds(pl.multiple_of(slot * rows, rows), rows)
    for tile in range(tiles):
        high, low = split(total[tile])
        a_high[at, tile * depth : (tile + 1) * depth] = high
        a_low[at, tile * depth : (tile + 1) * depth] = low

    @pl.when(slot == slots - 1)
    def _():
        features_copy.wait()

        def split_tile(tile, carry):
            high, low = split(features[tile])
            here = pl.ds(pl.multiple_of(tile * depth, depth), depth)
            f_high[here, :] = high
            f_low[here, :] = low
            return carry

        lax.fori_loop(0, tiles, split_tile, 0)
        width = min(feat, 2 * LANES)
        for n in range(0, feat, width):
            cut = slice(n, n + width)
            part = dot3(a_high[...], a_low[...], f_high[:, cut], f_low[:, cut])
            for g in range(slots):
                for t in range(0, width, LANES):
                    piece = part[g * rows : (g + 1) * rows, t : t + LANES]
                    place = (g * feat + n + t) // LANES
                    out_ref[:, place] = piece.reshape(peers, piece_rows, LANES)
        if with_ids:
            lane = lax.broadcasted_iota(I32, (peers, piece_rows, LANES), 2)
            ids = jnp.zeros((peers, piece_rows, LANES), I32)
            for g in range(slots):
                ids = jnp.where(lane == g, ids_ref[g], ids)
            out_ref[:, slots * feat // LANES] = ids.astype(F32)


def product(blocks, features, col_ids, row_ids, part, peers, with_ids):
    slots, rows, width = blocks.shape
    tiles, depth, feat = features.shape
    rows //= 2
    out = (peers, slots * feat // LANES + int(with_ids), rows // peers, LANES)
    return pl.pallas_call(
        functools.partial(product_kernel, with_ids),
        grid_spec=pltpu.PrefetchScalarGridSpec(
            num_scalar_prefetch=2,
            grid=(slots,),
            in_specs=[
                pl.BlockSpec((1, rows, width), lambda k, part, ids: (k, part[0], 0)),
                spec(pltpu.HBM),
                spec(pltpu.HBM),
            ],
            out_specs=pl.BlockSpec(out, lambda k, part, ids: (0, 0, 0, 0)),
            scratch_shapes=[
                pltpu.VMEM((tiles, rows, depth), F32),
                pltpu.VMEM((slots * rows, tiles * depth), BF16),
                pltpu.VMEM((slots * rows, tiles * depth), BF16),
                pltpu.VMEM((tiles * depth, feat), BF16),
                pltpu.VMEM((tiles * depth, feat), BF16),
                pltpu.VMEM(features.shape, F32),
                pltpu.SMEM(col_ids.shape, I32),
                pltpu.SemaphoreType.DMA((2,)),
            ],
        ),
        out_shape=jax.ShapeDtypeStruct(out, F32),
        compiler_params=params(),
        cost_estimate=pl.CostEstimate(
            flops=6 * slots * rows * tiles * depth * feat,
            bytes_accessed=4 * (slots * rows * width + tiles * depth * feat),
            transcendentals=0,
        ),
        name="product",
    )(part, row_ids, blocks, col_ids, features)


def sum_kernel(slots, pieces_ref, out_ref, ids_out, ids, sem):
    peers, places = pieces_ref.shape[:2]
    tiles = out_ref.shape[1]
    ids_copy = pltpu.make_async_copy(pieces_ref.at[:, places - 1], ids, sem)
    ids_copy.start()
    out_ref[...] = jnp.zeros_like(out_ref)
    ids_copy.wait()

    def add_peer(peer, carry):
        for slot in range(slots):
            row = ids[peer, 0, slot].astype(I32)
            ids_out[peer * slots + slot] = row
            out_ref[row] = out_ref[row] + pieces_ref[peer, slot * tiles : (slot + 1) * tiles]
        return carry

    lax.fori_loop(0, peers, add_peer, 0)


def sum_pieces(pieces, row_blocks, slots):
    peers, places, rows, _ = pieces.shape
    tiles = (places - 1) // slots
    return pl.pallas_call(
        functools.partial(sum_kernel, slots),
        in_specs=[spec(pltpu.VMEM)],
        out_specs=(spec(pltpu.VMEM), spec(pltpu.SMEM)),
        out_shape=(
            jax.ShapeDtypeStruct((row_blocks, tiles, rows, LANES), F32),
            jax.ShapeDtypeStruct((peers * slots,), I32),
        ),
        scratch_shapes=[pltpu.SMEM((peers, rows, LANES), F32), pltpu.SemaphoreType.DMA],
        compiler_params=params(),
        name="sum_pieces",
    )(pieces)


def update_kernel(slots, ids_ref, pieces_ref, got_ref, factor_ref, out_ref, total, left):
    peers = pieces_ref.shape[0]
    row_blocks, tiles, rows, _ = out_ref.shape
    total[...] = got_ref[...]

    def add_peer(peer, carry):
        for slot in range(slots):
            row = ids_ref[peer * slots + slot]
            total[row] = total[row] + pieces_ref[peer, slot * tiles : (slot + 1) * tiles]
        return carry

    lax.fori_loop(0, peers, add_peer, 0)
    for row in range(row_blocks):
        for t in range(tiles):
            left[row * rows : (row + 1) * rows, t * LANES : (t + 1) * LANES] = total[row, t]
    out = dot3(*split(jnp.tanh(left[...])), *split(factor_ref[...]))
    for row in range(row_blocks):
        for t in range(tiles):
            out_ref[row, t] = out[row * rows : (row + 1) * rows, t * LANES : (t + 1) * LANES]


def update(ids, pieces, got, factor, slots):
    row_blocks, tiles, rows, _ = got.shape
    return pl.pallas_call(
        functools.partial(update_kernel, slots),
        in_specs=[spec(pltpu.SMEM), spec(pltpu.VMEM), spec(pltpu.VMEM), spec(pltpu.VMEM)],
        out_specs=spec(pltpu.VMEM),
        out_shape=jax.ShapeDtypeStruct(got.shape, F32),
        scratch_shapes=[
            pltpu.VMEM(got.shape, F32),
            pltpu.VMEM((row_blocks * rows, tiles * LANES), F32),
        ],
        compiler_params=params(),
        name="update",
    )(ids, pieces, got, factor)


def answer_kernel(slots, ids_ref, half_ref, table_ref, out_ref):
    peers = out_ref.shape[0]
    tiles = table_ref.shape[1]
    first = half_ref[0] * peers

    def pick(peer, carry):
        for slot in range(slots):
            row = ids_ref[peer * slots + slot]
            out_ref[peer, slot * tiles : (slot + 1) * tiles] = table_ref[row]
        out_ref[peer, slots * tiles :] = table_ref[first + peer]
        return carry

    lax.fori_loop(0, peers, pick, 0)


def answer(ids, half, table, peers, slots):
    _, tiles, rows, _ = table.shape
    return pl.pallas_call(
        functools.partial(answer_kernel, slots),
        in_specs=[spec(pltpu.SMEM), spec(pltpu.SMEM), spec(pltpu.VMEM)],
        out_specs=spec(pltpu.VMEM),
        out_shape=jax.ShapeDtypeStruct((peers, (slots + 1) * tiles, rows, LANES), F32),
        compiler_params=params(),
        name="answer",
    )(ids, half, table)


def place_kernel(slots, part_ref, answers_ref, *refs):
    owned_ref, returned_ref = refs[-2:]
    peers, places, rows, _ = answers_ref.shape
    tiles = places // (slots + 1)

    def copy_out(peer, carry):
        here = pl.ds(peer * rows, rows)
        for t in range(tiles):
            cut = slice(t * LANES, (t + 1) * LANES)
            for slot in range(slots):
                returned_ref[slot, here, cut] = answers_ref[peer, slot * tiles + t]
            owned_ref[here, cut] = answers_ref[peer, slots * tiles + t]
        return carry

    for peer in range(peers):
        copy_out(peer, 0)


def place(part, answers, slots, earlier=()):
    peers, places, rows, _ = answers.shape
    feat = places // (slots + 1) * LANES
    half_rows = peers * rows
    return pl.pallas_call(
        functools.partial(place_kernel, slots),
        grid_spec=pltpu.PrefetchScalarGridSpec(
            num_scalar_prefetch=1,
            grid=(1,),
            in_specs=[pl.BlockSpec(answers.shape, lambda i, part: (0, 0, 0, 0))]
            + [spec(pltpu.HBM)] * len(earlier),
            out_specs=(
                pl.BlockSpec((half_rows, feat), lambda i, part: (part[0], 0)),
                pl.BlockSpec((slots, half_rows, feat), lambda i, part: (0, part[0], 0)),
            ),
        ),
        out_shape=(
            jax.ShapeDtypeStruct((2 * half_rows, feat), F32),
            jax.ShapeDtypeStruct((slots, 2 * half_rows, feat), F32),
        ),
        input_output_aliases={2 + i: i for i in range(len(earlier))},
        compiler_params=params(),
        name="place",
    )(part, answers, *earlier)


def local(axes, blocks, features, col_ids, row_ids, factor):
    half_axis, peer_axes = axes[0], axes[1:]
    slots, rows, _ = blocks.shape
    feat = features.shape[2]
    peers = lax.axis_size(peer_axes)
    row_blocks = peers * lax.axis_size(half_axis)
    here = lax.axis_index(half_axis).astype(I32).reshape(1)
    there = 1 - here
    swap = [(0, 1), (1, 0)]
    exchange = lambda pieces: lax.all_to_all(pieces, peer_axes, 0, 0)

    far = exchange(product(blocks, features, col_ids, row_ids, there, peers, True))
    near = exchange(product(blocks, features, col_ids, row_ids, here, peers, False))
    far_sums, ids = sum_pieces(far, row_blocks, slots)
    got = lax.ppermute(far_sums, half_axis, swap)
    near_rows = update(ids, near, got, factor, slots)
    far_rows = lax.ppermute(near_rows, half_axis, swap)
    near_answers = exchange(answer(ids, here, near_rows, peers, slots))
    far_answers = exchange(answer(ids, here, far_rows, peers, slots))
    outputs = place(here, near_answers, slots)
    owned_rows, returned = place(there, far_answers, slots, outputs)
    return owned_rows, returned.reshape(slots * rows, feat)


def solution(mesh):
    outer, inner = mesh.devices.shape
    devices = mesh.devices.reshape(2, outer // 2, inner)
    axes = ("half", "gx_low", "gy")
    split_mesh = Mesh(devices, axes)
    return jax.shard_map(
        functools.partial(local, axes),
        mesh=split_mesh,
        in_specs=(P(axes, None, None), P(axes, None, None), P(axes, None), P(axes), P()),
        out_specs=(P(axes, None), P(axes, None)),
        check_vma=False,
    )
```

```python
import functools

import jax
import jax.numpy as jnp
from jax import lax
from jax.experimental import pallas as pl
from jax.experimental.pallas import tpu as pltpu
from jax.sharding import Mesh
from jax.sharding import PartitionSpec as P

F32 = jnp.float32
BF16 = jnp.bfloat16
I32 = jnp.int32
LANES = 128
VMEM_BYTES = 24 << 20
PRODUCT_VMEM_BYTES = 60 << 20


def split(value):
    high = value.astype(BF16)
    return high, (value - high.astype(F32)).astype(BF16)


def dot3(a_high, a_low, b_high, b_low):
    dot = functools.partial(jnp.dot, preferred_element_type=F32)
    return dot(a_high, b_high) + dot(a_high, b_low) + dot(a_low, b_high)


def spec(space):
    return pl.BlockSpec(memory_space=space)


def params(vmem_bytes=VMEM_BYTES):
    return pltpu.CompilerParams(vmem_limit_bytes=vmem_bytes)


def product_kernel(
    with_ids, groups, feature_parts, part_ref, blocks_hbm, ids_hbm, cols_hbm, features_hbm, out_ref,
    blocks, total, left, f_high, f_low, features, ids, cols, block_sems, feature_sems, id_sems,
):
    slots, per_row = cols.shape
    tiles, depth, feat = features.shape
    rows = blocks.shape[1]
    peers, _, piece_rows, _ = out_ref.shape
    in_group = slots // groups
    height = in_group * rows
    part_tiles = tiles // feature_parts
    first = pl.multiple_of(part_ref[0] * rows, rows)
    block_copies = [
        pltpu.make_async_copy(
            blocks_hbm.at[k, pl.ds(first, rows)], blocks.at[k], block_sems.at[k]
        )
        for k in range(slots)
    ]
    feature_copies = [
        pltpu.make_async_copy(
            features_hbm.at[pl.ds(k * part_tiles, part_tiles)],
            features.at[pl.ds(k * part_tiles, part_tiles)],
            feature_sems.at[k],
        )
        for k in range(feature_parts)
    ]
    id_copies = [
        pltpu.make_async_copy(cols_hbm, cols, id_sems.at[0]),
        pltpu.make_async_copy(ids_hbm, ids, id_sems.at[1]),
    ]
    for copy in id_copies + block_copies[:in_group] + feature_copies + block_copies[in_group:]:
        copy.start()
    for copy in id_copies:
        copy.wait()

    def combine(group):
        for s in range(in_group):
            slot = group * in_group + s
            block_copies[slot].wait()
            total[s] = jnp.zeros_like(total[s])
            for j in range(per_row):
                tile = cols[slot, j]
                total[s, tile] = total[s, tile] + blocks[slot, :, j * depth : (j + 1) * depth]
            for tile in range(tiles):
                high, low = split(total[s, tile])
                cut = slice(tile * depth, (tile + 1) * depth)
                left[group % 2, s * rows : (s + 1) * rows, cut] = high
                left[group % 2, height + s * rows : height + (s + 1) * rows, cut] = low

    def multiply(group):
        width = min(feat, 2 * LANES)
        dot = functools.partial(jnp.dot, preferred_element_type=F32)
        for n in range(0, feat, width):
            cut = slice(n, n + width)
            both = dot(left[group % 2], f_high[:, cut])
            both = both[:height] + both[height:] + dot(left[group % 2, :height], f_low[:, cut])
            for s in range(in_group):
                for t in range(0, width, LANES):
                    piece = both[s * rows : (s + 1) * rows, t : t + LANES]
                    place = ((group * in_group + s) * feat + n + t) // LANES
                    out_ref[:, place] = piece.reshape(peers, piece_rows, LANES)

    def split_tile(tile, carry):
        high, low = split(features[tile])
        here = pl.ds(pl.multiple_of(tile * depth, depth), depth)
        f_high[here, :] = high
        f_low[here, :] = low
        return carry

    combine(0)
    for k in range(feature_parts):
        feature_copies[k].wait()
        lax.fori_loop(k * part_tiles, (k + 1) * part_tiles, split_tile, 0)
    for group in range(groups):
        if group + 1 < groups:
            combine(group + 1)
        multiply(group)
    if with_ids:
        lane = lax.broadcasted_iota(I32, (peers, piece_rows, LANES), 2)
        shown = jnp.zeros((peers, piece_rows, LANES), I32)
        for slot in range(slots):
            shown = jnp.where(lane == slot, ids[slot], shown)
        out_ref[:, slots * feat // LANES] = shown.astype(F32)


def product(blocks, features, col_ids, row_ids, part, peers, with_ids):
    slots, rows, width = blocks.shape
    tiles, depth, feat = features.shape
    rows //= 2
    groups = 2 if slots % 2 == 0 else 1
    feature_parts = 4 if tiles % 4 == 0 else 1
    height = slots // groups * rows
    out = (peers, slots * feat // LANES + int(with_ids), rows // peers, LANES)
    return pl.pallas_call(
        functools.partial(product_kernel, with_ids, groups, feature_parts),
        in_specs=[spec(pltpu.SMEM)] + [spec(pltpu.HBM)] * 4,
        out_specs=spec(pltpu.VMEM),
        out_shape=jax.ShapeDtypeStruct(out, F32),
        scratch_shapes=[
            pltpu.VMEM((slots, rows, width), F32),
            pltpu.VMEM((slots // groups, tiles, rows, depth), F32),
            pltpu.VMEM((2, 2 * height, tiles * depth), BF16),
            pltpu.VMEM((tiles * depth, feat), BF16),
            pltpu.VMEM((tiles * depth, feat), BF16),
            pltpu.VMEM(features.shape, F32),
            pltpu.SMEM(row_ids.shape, I32),
            pltpu.SMEM(col_ids.shape, I32),
            pltpu.SemaphoreType.DMA((slots,)),
            pltpu.SemaphoreType.DMA((feature_parts,)),
            pltpu.SemaphoreType.DMA((2,)),
        ],
        compiler_params=params(PRODUCT_VMEM_BYTES),
        cost_estimate=pl.CostEstimate(
            flops=6 * slots * rows * tiles * depth * feat,
            bytes_accessed=4 * (slots * rows * width + tiles * depth * feat),
            transcendentals=0,
        ),
        name="product",
    )(part, blocks, row_ids, col_ids, features)


def sum_kernel(slots, pieces_ref, out_ref, ids_out, ids, sem):
    peers, places = pieces_ref.shape[:2]
    tiles = out_ref.shape[1]
    ids_copy = pltpu.make_async_copy(pieces_ref.at[:, places - 1], ids, sem)
    ids_copy.start()
    out_ref[...] = jnp.zeros_like(out_ref)
    ids_copy.wait()

    def add_peer(peer, carry):
        for slot in range(slots):
            row = ids[peer, 0, slot].astype(I32)
            ids_out[peer * slots + slot] = row
            out_ref[row] = out_ref[row] + pieces_ref[peer, slot * tiles : (slot + 1) * tiles]
        return carry

    lax.fori_loop(0, peers, add_peer, 0)


def sum_pieces(pieces, row_blocks, slots):
    peers, places, rows, _ = pieces.shape
    tiles = (places - 1) // slots
    return pl.pallas_call(
        functools.partial(sum_kernel, slots),
        in_specs=[spec(pltpu.VMEM)],
        out_specs=(spec(pltpu.VMEM), spec(pltpu.SMEM)),
        out_shape=(
            jax.ShapeDtypeStruct((row_blocks, tiles, rows, LANES), F32),
            jax.ShapeDtypeStruct((peers * slots,), I32),
        ),
        scratch_shapes=[pltpu.SMEM((peers, rows, LANES), F32), pltpu.SemaphoreType.DMA],
        compiler_params=params(),
        name="sum_pieces",
    )(pieces)


def update_kernel(slots, ids_ref, pieces_ref, got_ref, factor_ref, out_ref, total, left):
    peers = pieces_ref.shape[0]
    row_blocks, tiles, rows, _ = out_ref.shape
    total[...] = got_ref[...]

    def add_peer(peer, carry):
        for slot in range(slots):
            row = ids_ref[peer * slots + slot]
            total[row] = total[row] + pieces_ref[peer, slot * tiles : (slot + 1) * tiles]
        return carry

    lax.fori_loop(0, peers, add_peer, 0)
    for row in range(row_blocks):
        for t in range(tiles):
            left[row * rows : (row + 1) * rows, t * LANES : (t + 1) * LANES] = total[row, t]
    out = dot3(*split(jnp.tanh(left[...])), *split(factor_ref[...]))
    for row in range(row_blocks):
        for t in range(tiles):
            out_ref[row, t] = out[row * rows : (row + 1) * rows, t * LANES : (t + 1) * LANES]


def update(ids, pieces, got, factor, slots):
    row_blocks, tiles, rows, _ = got.shape
    return pl.pallas_call(
        functools.partial(update_kernel, slots),
        in_specs=[spec(pltpu.SMEM), spec(pltpu.VMEM), spec(pltpu.VMEM), spec(pltpu.VMEM)],
        out_specs=spec(pltpu.VMEM),
        out_shape=jax.ShapeDtypeStruct(got.shape, F32),
        scratch_shapes=[
            pltpu.VMEM(got.shape, F32),
            pltpu.VMEM((row_blocks * rows, tiles * LANES), F32),
        ],
        compiler_params=params(),
        name="update",
    )(ids, pieces, got, factor)


def answer_kernel(slots, ids_ref, self_ref, mine_ref, mate_ref, *refs):
    out_ref, table = refs[-2:]
    chips = out_ref.shape[0]
    _, tiles, rows, _ = mine_ref.shape
    core, first = self_ref[1], self_ref[0] * chips * 2
    mine, mate = mine_ref[...], mate_ref[...]
    table[:, :, :rows] = jnp.where(core == 0, mine, mate)
    table[:, :, rows:] = jnp.where(core == 0, mate, mine)

    def pick(chip, carry):
        peer = chip * 2 + core
        for slot in range(slots):
            row = ids_ref[peer * slots + slot]
            out_ref[chip, 0, slot * tiles : (slot + 1) * tiles] = table[row]
        out_ref[chip, 0, slots * tiles :] = table[first + peer]
        return carry

    lax.fori_loop(0, chips, pick, 0)


def answer(ids, self_at, mine, mate, chips, slots, part, cost_bytes, earlier=()):
    row_blocks, tiles, rows, _ = mine.shape
    places = (slots + 1) * tiles
    block = (chips, 1, places, 2 * rows, LANES)
    return pl.pallas_call(
        functools.partial(answer_kernel, slots),
        in_specs=[spec(pltpu.SMEM), spec(pltpu.SMEM), spec(pltpu.VMEM), spec(pltpu.VMEM)]
        + [spec(pltpu.HBM)] * len(earlier),
        grid=(1,),
        out_specs=pl.BlockSpec(block, lambda i: (0, part, 0, 0, 0)),
        out_shape=jax.ShapeDtypeStruct((chips, 2, places, 2 * rows, LANES), F32),
        scratch_shapes=[pltpu.VMEM((row_blocks, tiles, 2 * rows, LANES), F32)],
        input_output_aliases={4 + i: i for i in range(len(earlier))},
        compiler_params=params(),
        cost_estimate=pl.CostEstimate(
            flops=cost_bytes << 14, bytes_accessed=cost_bytes, transcendentals=0
        ),
        name="answer",
    )(ids, self_at, mine, mate, *earlier)


def place_kernel(slots, parts_ref, answers_ref, owned_ref, returned_ref):
    chips, _, places, rows, _ = answers_ref.shape
    tiles = places // (slots + 1)
    for chip in range(chips):
        here = pl.ds(chip * rows, rows)
        for t in range(tiles):
            cut = slice(t * LANES, (t + 1) * LANES)
            for slot in range(slots):
                returned_ref[slot, here, cut] = answers_ref[chip, 0, slot * tiles + t]
            owned_ref[here, cut] = answers_ref[chip, 0, slots * tiles + t]


def place(parts, answers, slots):
    chips, _, places, rows, _ = answers.shape
    feat = places // (slots + 1) * LANES
    half_rows = chips * rows
    return pl.pallas_call(
        functools.partial(place_kernel, slots),
        grid_spec=pltpu.PrefetchScalarGridSpec(
            num_scalar_prefetch=1,
            grid=(2,),
            in_specs=[
                pl.BlockSpec((chips, 1, places, rows, LANES), lambda i, parts: (0, i, 0, 0, 0))
            ],
            out_specs=(
                pl.BlockSpec((half_rows, feat), lambda i, parts: (parts[i], 0)),
                pl.BlockSpec((slots, half_rows, feat), lambda i, parts: (0, parts[i], 0)),
            ),
        ),
        out_shape=(
            jax.ShapeDtypeStruct((2 * half_rows, feat), F32),
            jax.ShapeDtypeStruct((slots, 2 * half_rows, feat), F32),
        ),
        compiler_params=params(),
        name="place",
    )(parts, answers)


def local(blocks, features, col_ids, row_ids, factor):
    slots, rows, _ = blocks.shape
    feat = features.shape[2]
    chips = lax.axis_size("chip")
    peer_axes = ("chip", "core")
    peers = lax.axis_size(peer_axes)
    row_blocks = peers * lax.axis_size("half")
    half = lax.axis_index("half").astype(I32)
    here = half.reshape(1)
    there = 1 - here
    parts = jnp.concatenate([here, there])
    self_at = jnp.stack([half, lax.axis_index("core").astype(I32)])
    swap = [(0, 1), (1, 0)]
    parts, self_at, row_ids = lax.optimization_barrier((parts, self_at, row_ids))

    far = product(blocks, features, col_ids, row_ids, there, peers, True)
    far = lax.all_to_all(far, peer_axes, 0, 0)
    near = product(blocks, features, col_ids, row_ids, here, peers, False)
    near = lax.all_to_all(near, peer_axes, 0, 0)
    far_sums, ids = sum_pieces(far, row_blocks, slots)
    got = lax.ppermute(far_sums, "half", swap)
    near_rows = update(ids, near, got, factor, slots)

    far_rows = lax.ppermute(near_rows, "half", swap)
    near_mate = lax.ppermute(near_rows, "core", swap)
    answers = answer(ids, self_at, near_rows, near_mate, chips, slots, 0, 1 << 22)
    far_mate = lax.ppermute(far_rows, "core", swap)
    answers = answer(ids, self_at, far_rows, far_mate, chips, slots, 1, 1 << 20, (answers,))
    answers = lax.all_to_all(answers, "chip", 0, 0)
    owned_rows, returned = place(parts, answers, slots)
    return owned_rows, returned.reshape(slots * rows, feat)


def solution(mesh):
    devices = mesh.devices.reshape(2, mesh.devices.size // 4, 2)
    axes = ("half", "chip", "core")
    split_mesh = Mesh(devices, axes)
    return jax.shard_map(
        local,
        mesh=split_mesh,
        in_specs=(P(axes, None, None), P(axes, None, None), P(axes, None), P(axes), P()),
        out_specs=(P(axes, None), P(axes, None)),
        check_vma=False,
    )
```

```python
import functools

import jax
import jax.numpy as jnp
from jax import lax
from jax.experimental import pallas as pl
from jax.experimental.pallas import tpu as pltpu
from jax.sharding import Mesh
from jax.sharding import PartitionSpec as P

F32 = jnp.float32
BF16 = jnp.bfloat16
I32 = jnp.int32
LANES = 128
UNROLL = 8
VMEM_BYTES = 24 << 20
PRODUCT_VMEM_BYTES = 60 << 20


def split(value):
    high = value.astype(BF16)
    return high, (value - high.astype(F32)).astype(BF16)


def dot3(a_high, a_low, b_high, b_low):
    dot = functools.partial(jnp.dot, preferred_element_type=F32)
    return dot(a_high, b_high) + dot(a_high, b_low) + dot(a_low, b_high)


def spec(space):
    return pl.BlockSpec(memory_space=space)


def params(vmem_bytes=VMEM_BYTES):
    return pltpu.CompilerParams(vmem_limit_bytes=vmem_bytes)


def product_kernel(
    with_ids, groups, feature_parts, part_ref, blocks_hbm, ids_hbm, cols_hbm, features_hbm, out_ref,
    blocks, total, left, f_high, f_low, features, ids, cols, block_sems, feature_sems, id_sems,
):
    slots, per_row = cols.shape
    tiles, depth, feat = features.shape
    rows = blocks.shape[1]
    peers, _, piece_rows, _ = out_ref.shape
    in_group = slots // groups
    height = in_group * rows
    part_tiles = tiles // feature_parts
    first = pl.multiple_of(part_ref[0] * rows, rows)
    block_copies = [
        pltpu.make_async_copy(
            blocks_hbm.at[k, pl.ds(first, rows)], blocks.at[k], block_sems.at[k]
        )
        for k in range(slots)
    ]
    feature_copies = [
        pltpu.make_async_copy(
            features_hbm.at[pl.ds(k * part_tiles, part_tiles)],
            features.at[pl.ds(k * part_tiles, part_tiles)],
            feature_sems.at[k],
        )
        for k in range(feature_parts)
    ]
    id_copies = [
        pltpu.make_async_copy(cols_hbm, cols, id_sems.at[0]),
        pltpu.make_async_copy(ids_hbm, ids, id_sems.at[1]),
    ]
    for copy in id_copies + block_copies[:in_group] + feature_copies + block_copies[in_group:]:
        copy.start()
    for copy in id_copies:
        copy.wait()

    def combine(group):
        for s in range(in_group):
            slot = group * in_group + s
            block_copies[slot].wait()
            total[s] = jnp.zeros_like(total[s])
            for j in range(per_row):
                tile = cols[slot, j]
                total[s, tile] = total[s, tile] + blocks[slot, :, j * depth : (j + 1) * depth]
            for tile in range(tiles):
                high, low = split(total[s, tile])
                cut = slice(tile * depth, (tile + 1) * depth)
                left[group % 2, s * rows : (s + 1) * rows, cut] = high
                left[group % 2, height + s * rows : height + (s + 1) * rows, cut] = low

    def multiply(group):
        width = min(feat, 2 * LANES)
        dot = functools.partial(jnp.dot, preferred_element_type=F32)
        for n in range(0, feat, width):
            cut = slice(n, n + width)
            both = dot(left[group % 2], f_high[:, cut])
            both = both[:height] + both[height:] + dot(left[group % 2, :height], f_low[:, cut])
            for s in range(in_group):
                for t in range(0, width, LANES):
                    piece = both[s * rows : (s + 1) * rows, t : t + LANES]
                    place = ((group * in_group + s) * feat + n + t) // LANES
                    out_ref[:, place] = piece.reshape(peers, piece_rows, LANES)

    def split_tile(tile, carry):
        high, low = split(features[tile])
        here = pl.ds(pl.multiple_of(tile * depth, depth), depth)
        f_high[here, :] = high
        f_low[here, :] = low
        return carry

    combine(0)
    for k in range(feature_parts):
        feature_copies[k].wait()
        lax.fori_loop(k * part_tiles, (k + 1) * part_tiles, split_tile, 0)
    for group in range(groups):
        if group + 1 < groups:
            combine(group + 1)
        multiply(group)
    if with_ids:
        lane = lax.broadcasted_iota(I32, (peers, piece_rows, LANES), 2)
        shown = jnp.zeros((peers, piece_rows, LANES), I32)
        for slot in range(slots):
            shown = jnp.where(lane == slot, ids[slot], shown)
        out_ref[:, slots * feat // LANES] = shown.astype(F32)


def product(blocks, features, col_ids, row_ids, part, peers, with_ids):
    slots, rows, width = blocks.shape
    tiles, depth, feat = features.shape
    rows //= 2
    groups = 2 if slots % 2 == 0 else 1
    feature_parts = 4 if tiles % 4 == 0 else 1
    height = slots // groups * rows
    out = (peers, slots * feat // LANES + int(with_ids), rows // peers, LANES)
    return pl.pallas_call(
        functools.partial(product_kernel, with_ids, groups, feature_parts),
        in_specs=[spec(pltpu.SMEM)] + [spec(pltpu.HBM)] * 4,
        out_specs=spec(pltpu.VMEM),
        out_shape=jax.ShapeDtypeStruct(out, F32),
        scratch_shapes=[
            pltpu.VMEM((slots, rows, width), F32),
            pltpu.VMEM((slots // groups, tiles, rows, depth), F32),
            pltpu.VMEM((2, 2 * height, tiles * depth), BF16),
            pltpu.VMEM((tiles * depth, feat), BF16),
            pltpu.VMEM((tiles * depth, feat), BF16),
            pltpu.VMEM(features.shape, F32),
            pltpu.SMEM(row_ids.shape, I32),
            pltpu.SMEM(col_ids.shape, I32),
            pltpu.SemaphoreType.DMA((slots,)),
            pltpu.SemaphoreType.DMA((feature_parts,)),
            pltpu.SemaphoreType.DMA((2,)),
        ],
        compiler_params=params(PRODUCT_VMEM_BYTES),
        cost_estimate=pl.CostEstimate(
            flops=6 * slots * rows * tiles * depth * feat,
            bytes_accessed=4 * (slots * rows * width + tiles * depth * feat),
            transcendentals=0,
        ),
        name="product",
    )(part, blocks, row_ids, col_ids, features)


def add_by_row(row_of, pieces_ref, tables, slots):
    peers = pieces_ref.shape[0]
    tiles = tables[0].shape[1]

    def add_peer(peer, carry):
        for slot in range(slots):
            row = row_of(peer, slot)
            table = tables[slot % len(tables)]
            table[row] = table[row] + pieces_ref[peer, slot * tiles : (slot + 1) * tiles]
        return carry

    lax.fori_loop(0, peers, add_peer, 0, unroll=UNROLL)


def sum_kernel(slots, pieces_ref, out_ref, ids_out, other, ids, sem):
    ids_out[...] = pieces_ref[:, pieces_ref.shape[1] - 1].astype(I32)
    ids_copy = pltpu.make_async_copy(ids_out, ids, sem)
    ids_copy.start()
    out_ref[...] = jnp.zeros_like(out_ref)
    other[...] = jnp.zeros_like(other)
    ids_copy.wait()

    add_by_row(lambda peer, slot: ids[peer, 0, slot], pieces_ref, (out_ref, other), slots)
    out_ref[...] += other[...]


def sum_pieces(pieces, row_blocks, slots):
    peers, places, rows, _ = pieces.shape
    tiles = (places - 1) // slots
    return pl.pallas_call(
        functools.partial(sum_kernel, slots),
        in_specs=[spec(pltpu.VMEM)],
        out_specs=(spec(pltpu.VMEM), spec(pltpu.VMEM)),
        out_shape=(
            jax.ShapeDtypeStruct((row_blocks, tiles, rows, LANES), F32),
            jax.ShapeDtypeStruct((peers, rows, LANES), I32),
        ),
        scratch_shapes=[
            pltpu.VMEM((row_blocks, tiles, rows, LANES), F32),
            pltpu.SMEM((peers, rows, LANES), I32),
            pltpu.SemaphoreType.DMA,
        ],
        compiler_params=params(),
        name="sum_pieces",
    )(pieces)


def update_kernel(slots, ids_ref, pieces_ref, got_ref, factor_ref, out_ref, total, other, left):
    row_blocks, tiles, rows, _ = out_ref.shape
    total[...] = got_ref[...]
    other[...] = jnp.zeros_like(other)
    add_by_row(
        lambda peer, slot: ids_ref[peer * slots + slot], pieces_ref, (total, other), slots
    )
    for row in range(row_blocks):
        for t in range(tiles):
            here = slice(row * rows, (row + 1) * rows), slice(t * LANES, (t + 1) * LANES)
            left[here] = total[row, t] + other[row, t]
    out = dot3(*split(jnp.tanh(left[...])), *split(factor_ref[...]))
    for row in range(row_blocks):
        for t in range(tiles):
            out_ref[row, t] = out[row * rows : (row + 1) * rows, t * LANES : (t + 1) * LANES]


def update(ids, pieces, got, factor, slots):
    row_blocks, tiles, rows, _ = got.shape
    return pl.pallas_call(
        functools.partial(update_kernel, slots),
        in_specs=[spec(pltpu.SMEM), spec(pltpu.VMEM), spec(pltpu.VMEM), spec(pltpu.VMEM)],
        out_specs=spec(pltpu.VMEM),
        out_shape=jax.ShapeDtypeStruct(got.shape, F32),
        scratch_shapes=[
            pltpu.VMEM(got.shape, F32),
            pltpu.VMEM(got.shape, F32),
            pltpu.VMEM((row_blocks * rows, tiles * LANES), F32),
        ],
        compiler_params=params(),
        name="update",
    )(ids, pieces, got, factor)


def answer_kernel(slots, ids_ref, self_ref, mine_ref, mate_ref, *refs):
    out_ref, table = refs[-2:]
    chips = out_ref.shape[0]
    _, tiles, rows, _ = mine_ref.shape
    core, first = self_ref[1], self_ref[0] * chips * 2
    mine, mate = mine_ref[...], mate_ref[...]
    table[:, :, :rows] = jnp.where(core == 0, mine, mate)
    table[:, :, rows:] = jnp.where(core == 0, mate, mine)

    def pick(chip, carry):
        peer = chip * 2 + core
        for slot in range(slots):
            row = ids_ref[peer * slots + slot]
            out_ref[chip, 0, slot * tiles : (slot + 1) * tiles] = table[row]
        out_ref[chip, 0, slots * tiles :] = table[first + peer]
        return carry

    lax.fori_loop(0, chips, pick, 0, unroll=UNROLL)


def answer(ids, self_at, mine, mate, chips, slots, part, cost_bytes, earlier=()):
    row_blocks, tiles, rows, _ = mine.shape
    places = (slots + 1) * tiles
    block = (chips, 1, places, 2 * rows, LANES)
    return pl.pallas_call(
        functools.partial(answer_kernel, slots),
        in_specs=[spec(pltpu.SMEM), spec(pltpu.SMEM), spec(pltpu.VMEM), spec(pltpu.VMEM)]
        + [spec(pltpu.HBM)] * len(earlier),
        grid=(1,),
        out_specs=pl.BlockSpec(block, lambda i: (0, part, 0, 0, 0)),
        out_shape=jax.ShapeDtypeStruct((chips, 2, places, 2 * rows, LANES), F32),
        scratch_shapes=[pltpu.VMEM((row_blocks, tiles, 2 * rows, LANES), F32)],
        input_output_aliases={4 + i: i for i in range(len(earlier))},
        compiler_params=params(),
        cost_estimate=pl.CostEstimate(
            flops=cost_bytes << 14, bytes_accessed=cost_bytes, transcendentals=0
        ),
        name="answer",
    )(ids, self_at, mine, mate, *earlier)


def place_kernel(parts_ref, answers_ref, owned_hbm, returned_hbm, sems):
    chips, parts, places, _, _ = answers_ref.shape
    slots, _, tiles, _, _ = returned_hbm.shape
    copies = []
    for part in range(parts):
        at = pl.ds(parts_ref[part] * chips, chips)
        for place in range(slots + 1):
            source = answers_ref.at[:, part, place * tiles : (place + 1) * tiles]
            target = returned_hbm.at[place, at] if place < slots else owned_hbm.at[at]
            copies.append(pltpu.make_async_copy(source, target, sems.at[part, place]))
            copies[-1].start()
    for copy in copies:
        copy.wait()


def place(parts, answers, slots):
    chips, halves, places, rows, _ = answers.shape
    tiles = places // (slots + 1)
    owned = (halves * chips, tiles, rows, LANES)
    owned_rows, returned = pl.pallas_call(
        place_kernel,
        in_specs=[spec(pltpu.SMEM), spec(pl.ANY)],
        out_specs=(spec(pltpu.HBM), spec(pltpu.HBM)),
        out_shape=(
            jax.ShapeDtypeStruct(owned, F32),
            jax.ShapeDtypeStruct((slots, *owned), F32),
        ),
        scratch_shapes=[pltpu.SemaphoreType.DMA((halves, slots + 1))],
        compiler_params=params(),
        name="place",
    )(parts, answers)
    feat = tiles * LANES
    owned_rows = owned_rows.transpose(0, 2, 1, 3).reshape(-1, feat)
    returned = returned.transpose(0, 1, 3, 2, 4).reshape(-1, feat)
    return owned_rows, returned


def local(blocks, features, col_ids, row_ids, factor):
    slots = blocks.shape[0]
    chips = lax.axis_size("chip")
    peer_axes = ("chip", "core")
    peers = lax.axis_size(peer_axes)
    row_blocks = peers * lax.axis_size("half")
    half = lax.axis_index("half").astype(I32)
    here = half.reshape(1)
    there = 1 - here
    parts = jnp.concatenate([here, there])
    self_at = jnp.stack([half, lax.axis_index("core").astype(I32)])
    swap = [(0, 1), (1, 0)]
    parts, self_at, row_ids = lax.optimization_barrier((parts, self_at, row_ids))

    far = product(blocks, features, col_ids, row_ids, there, peers, True)
    far = lax.all_to_all(far, peer_axes, 0, 0)
    near = product(blocks, features, col_ids, row_ids, here, peers, False)
    near = lax.all_to_all(near, peer_axes, 0, 0)
    far_sums, ids = sum_pieces(far, row_blocks, slots)
    got = lax.ppermute(far_sums, "half", swap)
    ids = ids[:, 0, :slots].reshape(-1)
    near_rows = update(ids, near, got, factor, slots)

    far_rows = lax.ppermute(near_rows, "half", swap)
    near_mate = lax.ppermute(near_rows, "core", swap)
    answers = answer(ids, self_at, near_rows, near_mate, chips, slots, 0, 1 << 22)
    far_mate = lax.ppermute(far_rows, "core", swap)
    answers = answer(ids, self_at, far_rows, far_mate, chips, slots, 1, 1 << 20, (answers,))
    answers = lax.all_to_all(answers, "chip", 0, 0)
    return place(parts, answers, slots)


def solution(mesh):
    devices = mesh.devices.reshape(2, mesh.devices.size // 4, 2)
    axes = ("half", "chip", "core")
    split_mesh = Mesh(devices, axes)
    return jax.shard_map(
        local,
        mesh=split_mesh,
        in_specs=(P(axes, None, None), P(axes, None, None), P(axes, None), P(axes), P()),
        out_specs=(P(axes, None), P(axes, None)),
        check_vma=False,
    )
```

```python
import functools

import jax
import jax.numpy as jnp
from jax import lax
from jax.experimental import pallas as pl
from jax.experimental.pallas import tpu as pltpu
from jax.sharding import Mesh
from jax.sharding import PartitionSpec as P

F32 = jnp.float32
BF16 = jnp.bfloat16
I32 = jnp.int32
LANES = 128
UNROLL = 8
VMEM_BYTES = 24 << 20
PRODUCT_VMEM_BYTES = 60 << 20


def split(value):
    high = value.astype(BF16)
    return high, (value - high.astype(F32)).astype(BF16)


def dot3(a_high, a_low, b_high, b_low):
    dot = functools.partial(jnp.dot, preferred_element_type=F32)
    return dot(a_high, b_high) + dot(a_high, b_low) + dot(a_low, b_high)


def spec(space):
    return pl.BlockSpec(memory_space=space)


def params(vmem_bytes=VMEM_BYTES):
    return pltpu.CompilerParams(vmem_limit_bytes=vmem_bytes)


def product_kernel(
    with_ids, groups, feature_parts, part_ref, blocks_hbm, ids_hbm, cols_hbm, features_hbm, out_ref,
    blocks, total, left, f_high, f_low, features, ids, cols, block_sems, feature_sems, id_sems,
):
    slots, per_row = cols.shape
    tiles, depth, feat = features.shape
    rows = blocks.shape[1]
    peers, _, piece_rows, _ = out_ref.shape
    in_group = slots // groups
    height = in_group * rows
    part_tiles = tiles // feature_parts
    first = pl.multiple_of(part_ref[0] * rows, rows)
    block_copies = [
        pltpu.make_async_copy(
            blocks_hbm.at[k, pl.ds(first, rows)], blocks.at[k], block_sems.at[k]
        )
        for k in range(slots)
    ]
    feature_copies = [
        pltpu.make_async_copy(
            features_hbm.at[pl.ds(k * part_tiles, part_tiles)],
            features.at[pl.ds(k * part_tiles, part_tiles)],
            feature_sems.at[k],
        )
        for k in range(feature_parts)
    ]
    id_copies = [
        pltpu.make_async_copy(cols_hbm, cols, id_sems.at[0]),
        pltpu.make_async_copy(ids_hbm, ids, id_sems.at[1]),
    ]
    for copy in id_copies + block_copies[:in_group] + feature_copies + block_copies[in_group:]:
        copy.start()
    for copy in id_copies:
        copy.wait()

    def combine(group):
        for s in range(in_group):
            slot = group * in_group + s
            block_copies[slot].wait()
            total[s] = jnp.zeros_like(total[s])
            for j in range(per_row):
                tile = cols[slot, j]
                total[s, tile] = total[s, tile] + blocks[slot, :, j * depth : (j + 1) * depth]
            for tile in range(tiles):
                high, low = split(total[s, tile])
                cut = slice(tile * depth, (tile + 1) * depth)
                left[group % 2, s * rows : (s + 1) * rows, cut] = high
                left[group % 2, height + s * rows : height + (s + 1) * rows, cut] = low

    def multiply(group):
        width = min(feat, 2 * LANES)
        dot = functools.partial(jnp.dot, preferred_element_type=F32)
        for n in range(0, feat, width):
            cut = slice(n, n + width)
            both = dot(left[group % 2], f_high[:, cut])
            both = both[:height] + both[height:] + dot(left[group % 2, :height], f_low[:, cut])
            for s in range(in_group):
                for t in range(0, width, LANES):
                    piece = both[s * rows : (s + 1) * rows, t : t + LANES]
                    place = ((group * in_group + s) * feat + n + t) // LANES
                    piece = piece.reshape(peers // 2, 2, piece_rows, LANES)
                    out_ref[: peers // 2, place] = piece[:, 0]
                    out_ref[peers // 2 :, place] = piece[:, 1]

    def split_tile(tile, carry):
        high, low = split(features[tile])
        here = pl.ds(pl.multiple_of(tile * depth, depth), depth)
        f_high[here, :] = high
        f_low[here, :] = low
        return carry

    combine(0)
    for k in range(feature_parts):
        feature_copies[k].wait()
        lax.fori_loop(k * part_tiles, (k + 1) * part_tiles, split_tile, 0)
    for group in range(groups):
        if group + 1 < groups:
            combine(group + 1)
        multiply(group)
    if with_ids:
        lane = lax.broadcasted_iota(I32, (peers, piece_rows, LANES), 2)
        shown = jnp.zeros((peers, piece_rows, LANES), I32)
        for slot in range(slots):
            shown = jnp.where(lane == slot, ids[slot], shown)
        out_ref[:, slots * feat // LANES] = shown.astype(F32)


def product(blocks, features, col_ids, row_ids, part, peers, with_ids):
    slots, rows, width = blocks.shape
    tiles, depth, feat = features.shape
    rows //= 2
    groups = 2 if slots % 2 == 0 else 1
    feature_parts = 4 if tiles % 4 == 0 else 1
    height = slots // groups * rows
    out = (peers, slots * feat // LANES + int(with_ids), rows // peers, LANES)
    return pl.pallas_call(
        functools.partial(product_kernel, with_ids, groups, feature_parts),
        in_specs=[spec(pltpu.SMEM)] + [spec(pltpu.HBM)] * 4,
        out_specs=spec(pltpu.VMEM),
        out_shape=jax.ShapeDtypeStruct(out, F32),
        scratch_shapes=[
            pltpu.VMEM((slots, rows, width), F32),
            pltpu.VMEM((slots // groups, tiles, rows, depth), F32),
            pltpu.VMEM((2, 2 * height, tiles * depth), BF16),
            pltpu.VMEM((tiles * depth, feat), BF16),
            pltpu.VMEM((tiles * depth, feat), BF16),
            pltpu.VMEM(features.shape, F32),
            pltpu.SMEM(row_ids.shape, I32),
            pltpu.SMEM(col_ids.shape, I32),
            pltpu.SemaphoreType.DMA((slots,)),
            pltpu.SemaphoreType.DMA((feature_parts,)),
            pltpu.SemaphoreType.DMA((2,)),
        ],
        compiler_params=params(PRODUCT_VMEM_BYTES),
        cost_estimate=pl.CostEstimate(
            flops=6 * slots * rows * tiles * depth * feat,
            bytes_accessed=4 * (slots * rows * width + tiles * depth * feat),
            transcendentals=0,
        ),
        name="product",
    )(part, blocks, row_ids, col_ids, features)


def add_by_row(row_of, pieces_ref, tables, slots):
    peers = pieces_ref.shape[0]
    tiles = tables[0].shape[1]

    def add_peer(peer, carry):
        for slot in range(slots):
            row = row_of(peer, slot)
            table = tables[slot % len(tables)]
            table[row] = table[row] + pieces_ref[peer, slot * tiles : (slot + 1) * tiles]
        return carry

    lax.fori_loop(0, peers, add_peer, 0, unroll=UNROLL)


def sum_kernel(slots, pieces_ref, out_ref, ids_out, other, ids, sem):
    ids_out[...] = pieces_ref[:, pieces_ref.shape[1] - 1].astype(I32)
    ids_copy = pltpu.make_async_copy(ids_out, ids, sem)
    ids_copy.start()
    out_ref[...] = jnp.zeros_like(out_ref)
    other[...] = jnp.zeros_like(other)
    ids_copy.wait()

    add_by_row(lambda peer, slot: ids[peer, 0, slot], pieces_ref, (out_ref, other), slots)
    out_ref[...] += other[...]


def sum_pieces(pieces, row_blocks, slots):
    peers, places, rows, _ = pieces.shape
    tiles = (places - 1) // slots
    return pl.pallas_call(
        functools.partial(sum_kernel, slots),
        in_specs=[spec(pltpu.VMEM)],
        out_specs=(spec(pltpu.VMEM), spec(pltpu.VMEM)),
        out_shape=(
            jax.ShapeDtypeStruct((row_blocks, tiles, rows, LANES), F32),
            jax.ShapeDtypeStruct((peers, rows, LANES), I32),
        ),
        scratch_shapes=[
            pltpu.VMEM((row_blocks, tiles, rows, LANES), F32),
            pltpu.SMEM((peers, rows, LANES), I32),
            pltpu.SemaphoreType.DMA,
        ],
        compiler_params=params(),
        name="sum_pieces",
    )(pieces)


def update_kernel(slots, ids_ref, pieces_ref, got_ref, factor_ref, out_ref, total, other, left):
    row_blocks, tiles, rows, _ = out_ref.shape
    total[...] = got_ref[...]
    other[...] = jnp.zeros_like(other)
    add_by_row(
        lambda peer, slot: ids_ref[peer * slots + slot], pieces_ref, (total, other), slots
    )
    for row in range(row_blocks):
        for t in range(tiles):
            here = slice(row * rows, (row + 1) * rows), slice(t * LANES, (t + 1) * LANES)
            left[here] = total[row, t] + other[row, t]
    out = dot3(*split(jnp.tanh(left[...])), *split(factor_ref[...]))
    for row in range(row_blocks):
        for t in range(tiles):
            out_ref[row, t] = out[row * rows : (row + 1) * rows, t * LANES : (t + 1) * LANES]


def update(ids, pieces, got, factor, slots):
    row_blocks, tiles, rows, _ = got.shape
    return pl.pallas_call(
        functools.partial(update_kernel, slots),
        in_specs=[spec(pltpu.SMEM), spec(pltpu.VMEM), spec(pltpu.VMEM), spec(pltpu.VMEM)],
        out_specs=spec(pltpu.VMEM),
        out_shape=jax.ShapeDtypeStruct(got.shape, F32),
        scratch_shapes=[
            pltpu.VMEM(got.shape, F32),
            pltpu.VMEM(got.shape, F32),
            pltpu.VMEM((row_blocks * rows, tiles * LANES), F32),
        ],
        compiler_params=params(),
        name="update",
    )(ids, pieces, got, factor)


def answer_kernel(slots, ids_ref, self_ref, mine_ref, mate_ref, *refs):
    out_ref, table = refs[-2:]
    chips = out_ref.shape[0]
    _, tiles, rows, _ = mine_ref.shape
    core, first = self_ref[1], self_ref[0] * chips * 2
    mine, mate = mine_ref[...], mate_ref[...]
    table[:, :, :rows] = jnp.where(core == 0, mine, mate)
    table[:, :, rows:] = jnp.where(core == 0, mate, mine)

    def pick(chip, carry):
        peer = core * chips + chip
        for slot in range(slots):
            row = ids_ref[peer * slots + slot]
            out_ref[chip, 0, slot * tiles : (slot + 1) * tiles] = table[row]
        out_ref[chip, 0, slots * tiles :] = table[first + chip * 2 + core]
        return carry

    lax.fori_loop(0, chips, pick, 0, unroll=UNROLL)


def answer(ids, self_at, mine, mate, chips, slots, part, cost_bytes, earlier=()):
    row_blocks, tiles, rows, _ = mine.shape
    places = (slots + 1) * tiles
    block = (chips, 1, places, 2 * rows, LANES)
    return pl.pallas_call(
        functools.partial(answer_kernel, slots),
        in_specs=[spec(pltpu.SMEM), spec(pltpu.SMEM), spec(pltpu.VMEM), spec(pltpu.VMEM)]
        + [spec(pltpu.HBM)] * len(earlier),
        grid=(1,),
        out_specs=pl.BlockSpec(block, lambda i: (0, part, 0, 0, 0)),
        out_shape=jax.ShapeDtypeStruct((chips, 2, places, 2 * rows, LANES), F32),
        scratch_shapes=[pltpu.VMEM((row_blocks, tiles, 2 * rows, LANES), F32)],
        input_output_aliases={4 + i: i for i in range(len(earlier))},
        compiler_params=params(),
        cost_estimate=pl.CostEstimate(
            flops=cost_bytes << 14, bytes_accessed=cost_bytes, transcendentals=0
        ),
        name="answer",
    )(ids, self_at, mine, mate, *earlier)


def place_kernel(parts_ref, answers_ref, owned_hbm, returned_hbm, sems):
    chips, parts, places, _, _ = answers_ref.shape
    slots, _, tiles, _, _ = returned_hbm.shape
    copies = []
    for part in range(parts):
        at = pl.ds(parts_ref[part] * chips, chips)
        for place in range(slots + 1):
            source = answers_ref.at[:, part, place * tiles : (place + 1) * tiles]
            target = returned_hbm.at[place, at] if place < slots else owned_hbm.at[at]
            copies.append(pltpu.make_async_copy(source, target, sems.at[part, place]))
            copies[-1].start()
    for copy in copies:
        copy.wait()


def place(parts, answers, slots):
    chips, halves, places, rows, _ = answers.shape
    tiles = places // (slots + 1)
    owned = (halves * chips, tiles, rows, LANES)
    owned_rows, returned = pl.pallas_call(
        place_kernel,
        in_specs=[spec(pltpu.SMEM), spec(pl.ANY)],
        out_specs=(spec(pltpu.HBM), spec(pltpu.HBM)),
        out_shape=(
            jax.ShapeDtypeStruct(owned, F32),
            jax.ShapeDtypeStruct((slots, *owned), F32),
        ),
        scratch_shapes=[pltpu.SemaphoreType.DMA((halves, slots + 1))],
        compiler_params=params(),
        name="place",
    )(parts, answers)
    feat = tiles * LANES
    owned_rows = owned_rows.transpose(0, 2, 1, 3).reshape(-1, feat)
    returned = returned.transpose(0, 1, 3, 2, 4).reshape(-1, feat)
    return owned_rows, returned


def local(blocks, features, col_ids, row_ids, factor):
    slots = blocks.shape[0]
    chips = lax.axis_size("chip")
    peer_axes = ("core", "chip")
    peers = lax.axis_size(peer_axes)
    row_blocks = peers * lax.axis_size("half")
    half = lax.axis_index("half").astype(I32)
    here = half.reshape(1)
    there = 1 - here
    parts = jnp.concatenate([here, there])
    self_at = jnp.stack([half, lax.axis_index("core").astype(I32)])
    swap = [(0, 1), (1, 0)]
    parts, self_at, row_ids = lax.optimization_barrier((parts, self_at, row_ids))

    far = product(blocks, features, col_ids, row_ids, there, peers, True)
    far = lax.all_to_all(far, peer_axes, 0, 0)
    near = product(blocks, features, col_ids, row_ids, here, peers, False)
    near = lax.all_to_all(near, peer_axes, 0, 0)
    far_sums, ids = sum_pieces(far, row_blocks, slots)
    got = lax.ppermute(far_sums, "half", swap)
    ids = ids[:, 0, :slots].reshape(-1)
    near_rows = update(ids, near, got, factor, slots)

    far_rows = lax.ppermute(near_rows, "half", swap)
    near_mate = lax.ppermute(near_rows, "core", swap)
    answers = answer(ids, self_at, near_rows, near_mate, chips, slots, 0, 1 << 22)
    far_mate = lax.ppermute(far_rows, "core", swap)
    answers = answer(ids, self_at, far_rows, far_mate, chips, slots, 1, 1 << 20, (answers,))
    answers = lax.all_to_all(answers, "chip", 0, 0)
    return place(parts, answers, slots)


def solution(mesh):
    devices = mesh.devices.reshape(2, mesh.devices.size // 4, 2)
    axes = ("half", "chip", "core")
    split_mesh = Mesh(devices, axes)
    return jax.shard_map(
        local,
        mesh=split_mesh,
        in_specs=(P(axes, None, None), P(axes, None, None), P(axes, None), P(axes), P()),
        out_specs=(P(axes, None), P(axes, None)),
        check_vma=False,
    )
```

```python
import functools

import jax
import jax.numpy as jnp
from jax import lax
from jax.experimental import pallas as pl
from jax.experimental.pallas import tpu as pltpu
from jax.sharding import Mesh
from jax.sharding import PartitionSpec as P

F32 = jnp.float32
BF16 = jnp.bfloat16
I32 = jnp.int32
LANES = 128
UNROLL = 8
VMEM_BYTES = 24 << 20
PRODUCT_VMEM_BYTES = 60 << 20


def split(value):
    high = value.astype(BF16)
    return high, (value - high.astype(F32)).astype(BF16)


def dot3(a_high, a_low, b_high, b_low):
    dot = functools.partial(jnp.dot, preferred_element_type=F32)
    return dot(a_high, b_high) + dot(a_high, b_low) + dot(a_low, b_high)


def spec(space):
    return pl.BlockSpec(memory_space=space)


def params(vmem_bytes=VMEM_BYTES):
    return pltpu.CompilerParams(vmem_limit_bytes=vmem_bytes)


def product_kernel(
    with_ids, groups, feature_parts, part_ref, blocks_hbm, ids_hbm, cols_hbm, features_hbm, out_ref,
    blocks, total, left, f_high, f_low, features, ids, cols, block_sems, feature_sems, id_sems,
):
    slots, per_row = cols.shape
    tiles, depth, feat = features.shape
    rows = blocks.shape[1]
    peers, _, piece_rows, _ = out_ref.shape
    in_group = slots // groups
    height = in_group * rows
    part_tiles = tiles // feature_parts
    first = pl.multiple_of(part_ref[0] * rows, rows)
    block_copies = [
        pltpu.make_async_copy(
            blocks_hbm.at[k, pl.ds(first, rows)], blocks.at[k], block_sems.at[k]
        )
        for k in range(slots)
    ]
    feature_copies = [
        pltpu.make_async_copy(
            features_hbm.at[pl.ds(k * part_tiles, part_tiles)],
            features.at[pl.ds(k * part_tiles, part_tiles)],
            feature_sems.at[k],
        )
        for k in range(feature_parts)
    ]
    id_copies = [
        pltpu.make_async_copy(cols_hbm, cols, id_sems.at[0]),
        pltpu.make_async_copy(ids_hbm, ids, id_sems.at[1]),
    ]
    for copy in id_copies + block_copies[:in_group] + feature_copies + block_copies[in_group:]:
        copy.start()
    for copy in id_copies:
        copy.wait()

    def combine(group):
        for s in range(in_group):
            slot = group * in_group + s
            block_copies[slot].wait()
            total[s] = jnp.zeros_like(total[s])
            for j in range(per_row):
                tile = cols[slot, j]
                total[s, tile] = total[s, tile] + blocks[slot, :, j * depth : (j + 1) * depth]
            for tile in range(tiles):
                high, low = split(total[s, tile])
                cut = slice(tile * depth, (tile + 1) * depth)
                left[group % 2, s * rows : (s + 1) * rows, cut] = high
                left[group % 2, height + s * rows : height + (s + 1) * rows, cut] = low

    def multiply(group):
        width = min(feat, 2 * LANES)
        dot = functools.partial(jnp.dot, preferred_element_type=F32)
        for n in range(0, feat, width):
            cut = slice(n, n + width)
            both = dot(left[group % 2], f_high[:, cut])
            both = both[:height] + both[height:] + dot(left[group % 2, :height], f_low[:, cut])
            for s in range(in_group):
                for t in range(0, width, LANES):
                    piece = both[s * rows : (s + 1) * rows, t : t + LANES]
                    place = ((group * in_group + s) * feat + n + t) // LANES
                    piece = piece.reshape(peers // 2, 2, piece_rows, LANES)
                    out_ref[: peers // 2, place] = piece[:, 0]
                    out_ref[peers // 2 :, place] = piece[:, 1]

    def split_tile(tile, carry):
        high, low = split(features[tile])
        here = pl.ds(pl.multiple_of(tile * depth, depth), depth)
        f_high[here, :] = high
        f_low[here, :] = low
        return carry

    combine(0)
    for k in range(feature_parts):
        feature_copies[k].wait()
        lax.fori_loop(k * part_tiles, (k + 1) * part_tiles, split_tile, 0)
    for group in range(groups):
        if group + 1 < groups:
            combine(group + 1)
        multiply(group)
    if with_ids:
        lane = lax.broadcasted_iota(I32, (peers, piece_rows, LANES), 2)
        shown = jnp.zeros((peers, piece_rows, LANES), I32)
        for slot in range(slots):
            shown = jnp.where(lane == slot, ids[slot], shown)
        out_ref[:, slots * feat // LANES] = shown.astype(F32)


def product(blocks, features, col_ids, row_ids, part, peers, with_ids):
    slots, rows, width = blocks.shape
    tiles, depth, feat = features.shape
    rows //= 2
    groups = 2 if slots % 2 == 0 else 1
    feature_parts = 4 if tiles % 4 == 0 else 1
    height = slots // groups * rows
    out = (peers, slots * feat // LANES + int(with_ids), rows // peers, LANES)
    return pl.pallas_call(
        functools.partial(product_kernel, with_ids, groups, feature_parts),
        in_specs=[spec(pltpu.SMEM)] + [spec(pltpu.HBM)] * 4,
        out_specs=spec(pltpu.VMEM),
        out_shape=jax.ShapeDtypeStruct(out, F32),
        scratch_shapes=[
            pltpu.VMEM((slots, rows, width), F32),
            pltpu.VMEM((slots // groups, tiles, rows, depth), F32),
            pltpu.VMEM((2, 2 * height, tiles * depth), BF16),
            pltpu.VMEM((tiles * depth, feat), BF16),
            pltpu.VMEM((tiles * depth, feat), BF16),
            pltpu.VMEM(features.shape, F32),
            pltpu.SMEM(row_ids.shape, I32),
            pltpu.SMEM(col_ids.shape, I32),
            pltpu.SemaphoreType.DMA((slots,)),
            pltpu.SemaphoreType.DMA((feature_parts,)),
            pltpu.SemaphoreType.DMA((2,)),
        ],
        compiler_params=params(PRODUCT_VMEM_BYTES),
        cost_estimate=pl.CostEstimate(
            flops=6 * slots * rows * tiles * depth * feat,
            bytes_accessed=4 * (slots * rows * width + tiles * depth * feat),
            transcendentals=0,
        ),
        name="product",
    )(part, blocks, row_ids, col_ids, features)


def add_by_row(row_of, pieces_ref, tables, slots):
    peers = pieces_ref.shape[0]
    tiles = tables[0].shape[1]

    def add_peer(peer, carry):
        for slot in range(slots):
            row = row_of(peer, slot)
            table = tables[slot % len(tables)]
            table[row] = table[row] + pieces_ref[peer, slot * tiles : (slot + 1) * tiles]
        return carry

    lax.fori_loop(0, peers, add_peer, 0, unroll=UNROLL)


def sum_kernel(slots, pieces_ref, out_ref, ids_out, other, ids, sem):
    ids_out[...] = pieces_ref[:, pieces_ref.shape[1] - 1].astype(I32)
    ids_copy = pltpu.make_async_copy(ids_out, ids, sem)
    ids_copy.start()
    out_ref[...] = jnp.zeros_like(out_ref)
    other[...] = jnp.zeros_like(other)
    ids_copy.wait()

    add_by_row(lambda peer, slot: ids[peer, 0, slot], pieces_ref, (out_ref, other), slots)
    out_ref[...] += other[...]


def sum_pieces(pieces, row_blocks, slots):
    peers, places, rows, _ = pieces.shape
    tiles = (places - 1) // slots
    return pl.pallas_call(
        functools.partial(sum_kernel, slots),
        in_specs=[spec(pltpu.VMEM)],
        out_specs=(spec(pltpu.VMEM), spec(pltpu.VMEM)),
        out_shape=(
            jax.ShapeDtypeStruct((row_blocks, tiles, rows, LANES), F32),
            jax.ShapeDtypeStruct((peers, rows, LANES), I32),
        ),
        scratch_shapes=[
            pltpu.VMEM((row_blocks, tiles, rows, LANES), F32),
            pltpu.SMEM((peers, rows, LANES), I32),
            pltpu.SemaphoreType.DMA,
        ],
        compiler_params=params(),
        name="sum_pieces",
    )(pieces)


def update_kernel(slots, ids_ref, pieces_ref, got_ref, factor_ref, out_ref, total, other, left):
    row_blocks, tiles, rows, _ = out_ref.shape
    total[...] = got_ref[...]
    other[...] = jnp.zeros_like(other)
    add_by_row(
        lambda peer, slot: ids_ref[peer * slots + slot], pieces_ref, (total, other), slots
    )
    for row in range(row_blocks):
        for t in range(tiles):
            here = slice(row * rows, (row + 1) * rows), slice(t * LANES, (t + 1) * LANES)
            left[here] = total[row, t] + other[row, t]
    out = dot3(*split(jnp.tanh(left[...])), *split(factor_ref[...]))
    for row in range(row_blocks):
        for t in range(tiles):
            out_ref[row, t] = out[row * rows : (row + 1) * rows, t * LANES : (t + 1) * LANES]


def update(ids, pieces, got, factor, slots):
    row_blocks, tiles, rows, _ = got.shape
    return pl.pallas_call(
        functools.partial(update_kernel, slots),
        in_specs=[spec(pltpu.SMEM), spec(pltpu.VMEM), spec(pltpu.VMEM), spec(pltpu.VMEM)],
        out_specs=spec(pltpu.VMEM),
        out_shape=jax.ShapeDtypeStruct(got.shape, F32),
        scratch_shapes=[
            pltpu.VMEM(got.shape, F32),
            pltpu.VMEM(got.shape, F32),
            pltpu.VMEM((row_blocks * rows, tiles * LANES), F32),
        ],
        compiler_params=params(),
        name="update",
    )(ids, pieces, got, factor)


def answer_kernel(slots, ids_ref, half_ref, table_ref, *refs):
    out_ref = refs[-1]
    peers = out_ref.shape[0]
    tiles = table_ref.shape[1]
    chips = peers // 2
    first = half_ref[0] * peers

    def pick(chip, carry):
        for core in range(2):
            peer = core * chips + chip
            for slot in range(slots):
                row = ids_ref[peer * slots + slot]
                out_ref[peer, 0, slot * tiles : (slot + 1) * tiles] = table_ref[row]
            out_ref[peer, 0, slots * tiles :] = table_ref[first + chip * 2 + core]
        return carry

    lax.fori_loop(0, chips, pick, 0, unroll=UNROLL)


def answer(ids, half, table, peers, slots, part, earlier=()):
    _, tiles, rows, _ = table.shape
    places = (slots + 1) * tiles
    block = (peers, 1, places, rows, LANES)
    return pl.pallas_call(
        functools.partial(answer_kernel, slots),
        in_specs=[spec(pltpu.SMEM), spec(pltpu.SMEM), spec(pltpu.VMEM)]
        + [spec(pltpu.HBM)] * len(earlier),
        grid=(1,),
        out_specs=pl.BlockSpec(block, lambda i: (0, part, 0, 0, 0)),
        out_shape=jax.ShapeDtypeStruct((peers, 2, places, rows, LANES), F32),
        input_output_aliases={3 + i: i for i in range(len(earlier))},
        compiler_params=params(),
        cost_estimate=pl.CostEstimate(
            flops=0, bytes_accessed=8 * peers * places * rows * LANES, transcendentals=0
        ),
        name="answer",
    )(ids, half, table, *earlier)


def place_kernel(slots, parts_ref, answers_ref, owned_hbm, returned_hbm, whole, sems):
    peers, parts, places, rows, _ = answers_ref.shape
    chips = peers // 2
    tiles = places // (slots + 1)
    copies = []
    for part in range(parts):
        at = pl.ds(parts_ref[part] * chips, chips)
        for place in range(slots + 1):
            cut = slice(place * tiles, (place + 1) * tiles)
            for core in range(2):
                whole[part, place, :, :, core * rows : (core + 1) * rows] = answers_ref[
                    core * chips : (core + 1) * chips, part, cut
                ]
            target = returned_hbm.at[place, at] if place < slots else owned_hbm.at[at]
            copies.append(
                pltpu.make_async_copy(whole.at[part, place], target, sems.at[part, place])
            )
            copies[-1].start()
    for copy in copies:
        copy.wait()


def place(parts, answers, slots):
    peers, halves, places, rows, _ = answers.shape
    chips = peers // 2
    tiles = places // (slots + 1)
    owned = (halves * chips, tiles, 2 * rows, LANES)
    owned_rows, returned = pl.pallas_call(
        functools.partial(place_kernel, slots),
        in_specs=[spec(pltpu.SMEM), spec(pltpu.VMEM)],
        out_specs=(spec(pltpu.HBM), spec(pltpu.HBM)),
        out_shape=(
            jax.ShapeDtypeStruct(owned, F32),
            jax.ShapeDtypeStruct((slots, *owned), F32),
        ),
        scratch_shapes=[
            pltpu.VMEM((halves, slots + 1, chips, tiles, 2 * rows, LANES), F32),
            pltpu.SemaphoreType.DMA((halves, slots + 1)),
        ],
        compiler_params=params(),
        name="place",
    )(parts, answers)
    feat = tiles * LANES
    owned_rows = owned_rows.transpose(0, 2, 1, 3).reshape(-1, feat)
    returned = returned.transpose(0, 1, 3, 2, 4).reshape(-1, feat)
    return owned_rows, returned


def local(blocks, features, col_ids, row_ids, factor):
    slots = blocks.shape[0]
    peer_axes = ("core", "chip")
    peers = lax.axis_size(peer_axes)
    row_blocks = peers * lax.axis_size("half")
    here = lax.axis_index("half").astype(I32).reshape(1)
    there = 1 - here
    parts = jnp.concatenate([here, there])
    swap = [(0, 1), (1, 0)]
    parts, here, row_ids = lax.optimization_barrier((parts, here, row_ids))

    far = product(blocks, features, col_ids, row_ids, there, peers, True)
    far = lax.all_to_all(far, peer_axes, 0, 0)
    near = product(blocks, features, col_ids, row_ids, here, peers, False)
    near = lax.all_to_all(near, peer_axes, 0, 0)
    far_sums, ids = sum_pieces(far, row_blocks, slots)
    got = lax.ppermute(far_sums, "half", swap)
    ids = ids[:, 0, :slots].reshape(-1)
    near_rows = update(ids, near, got, factor, slots)

    far_rows = lax.ppermute(near_rows, "half", swap)
    answers = answer(ids, here, near_rows, peers, slots, 0)
    answers = answer(ids, here, far_rows, peers, slots, 1, (answers,))
    answers = lax.all_to_all(answers, peer_axes, 0, 0)
    return place(parts, answers, slots)


def solution(mesh):
    devices = mesh.devices.reshape(2, mesh.devices.size // 4, 2)
    axes = ("half", "chip", "core")
    split_mesh = Mesh(devices, axes)
    return jax.shard_map(
        local,
        mesh=split_mesh,
        in_specs=(P(axes, None, None), P(axes, None, None), P(axes, None), P(axes), P()),
        out_specs=(P(axes, None), P(axes, None)),
        check_vma=False,
    )
```

```python
import functools

import jax
import jax.numpy as jnp
from jax import lax
from jax.experimental import pallas as pl
from jax.experimental.pallas import tpu as pltpu
from jax.sharding import Mesh
from jax.sharding import PartitionSpec as P

F32 = jnp.float32
BF16 = jnp.bfloat16
I32 = jnp.int32
LANES = 128
UNROLL = 8
VMEM_BYTES = 24 << 20
PRODUCT_VMEM_BYTES = 60 << 20


def split(value):
    high = value.astype(BF16)
    return high, (value - high.astype(F32)).astype(BF16)


def dot3(a_high, a_low, b_high, b_low):
    dot = functools.partial(jnp.dot, preferred_element_type=F32)
    return dot(a_high, b_high) + dot(a_high, b_low) + dot(a_low, b_high)


def spec(space):
    return pl.BlockSpec(memory_space=space)


def params(vmem_bytes=VMEM_BYTES):
    return pltpu.CompilerParams(vmem_limit_bytes=vmem_bytes)


def product_kernel(
    with_ids, groups, feature_parts, part_ref, blocks_hbm, ids_hbm, cols_hbm, features_hbm, out_ref,
    blocks, total, left, f_high, f_low, features, ids, cols, block_sems, feature_sems, id_sems,
):
    slots, per_row = cols.shape
    tiles, depth, feat = features.shape
    rows = blocks.shape[1]
    peers, _, piece_rows, _ = out_ref.shape
    in_group = slots // groups
    height = in_group * rows
    part_tiles = tiles // feature_parts
    first = pl.multiple_of(part_ref[0] * rows, rows)
    block_copies = [
        pltpu.make_async_copy(
            blocks_hbm.at[k, pl.ds(first, rows)], blocks.at[k], block_sems.at[k]
        )
        for k in range(slots)
    ]
    feature_copies = [
        pltpu.make_async_copy(
            features_hbm.at[pl.ds(k * part_tiles, part_tiles)],
            features.at[pl.ds(k * part_tiles, part_tiles)],
            feature_sems.at[k],
        )
        for k in range(feature_parts)
    ]
    id_copies = [
        pltpu.make_async_copy(cols_hbm, cols, id_sems.at[0]),
        pltpu.make_async_copy(ids_hbm, ids, id_sems.at[1]),
    ]
    for copy in id_copies + block_copies[:in_group] + feature_copies + block_copies[in_group:]:
        copy.start()
    for copy in id_copies:
        copy.wait()

    def combine(group):
        for s in range(in_group):
            slot = group * in_group + s
            block_copies[slot].wait()
            total[s] = jnp.zeros_like(total[s])
            for j in range(per_row):
                tile = cols[slot, j]
                total[s, tile] = total[s, tile] + blocks[slot, :, j * depth : (j + 1) * depth]
            for tile in range(tiles):
                high, low = split(total[s, tile])
                cut = slice(tile * depth, (tile + 1) * depth)
                left[group % 2, s * rows : (s + 1) * rows, cut] = high
                left[group % 2, height + s * rows : height + (s + 1) * rows, cut] = low

    def multiply(group):
        width = min(feat, 2 * LANES)
        dot = functools.partial(jnp.dot, preferred_element_type=F32)
        for n in range(0, feat, width):
            cut = slice(n, n + width)
            both = dot(left[group % 2], f_high[:, cut])
            both = both[:height] + both[height:] + dot(left[group % 2, :height], f_low[:, cut])
            for s in range(in_group):
                for t in range(0, width, LANES):
                    piece = both[s * rows : (s + 1) * rows, t : t + LANES]
                    place = ((group * in_group + s) * feat + n + t) // LANES
                    piece = piece.reshape(peers // 2, 2, piece_rows, LANES)
                    out_ref[: peers // 2, place] = piece[:, 0]
                    out_ref[peers // 2 :, place] = piece[:, 1]

    def split_tile(tile, carry):
        high, low = split(features[tile])
        here = pl.ds(pl.multiple_of(tile * depth, depth), depth)
        f_high[here, :] = high
        f_low[here, :] = low
        return carry

    combine(0)
    for k in range(feature_parts):
        feature_copies[k].wait()
        lax.fori_loop(k * part_tiles, (k + 1) * part_tiles, split_tile, 0)
    for group in range(groups):
        if group + 1 < groups:
            combine(group + 1)
        multiply(group)
    if with_ids:
        lane = lax.broadcasted_iota(I32, (peers, piece_rows, LANES), 2)
        shown = jnp.zeros((peers, piece_rows, LANES), I32)
        for slot in range(slots):
            shown = jnp.where(lane == slot, ids[slot], shown)
        out_ref[:, slots * feat // LANES] = shown.astype(F32)


def product(blocks, features, col_ids, row_ids, part, peers, with_ids):
    slots, rows, width = blocks.shape
    tiles, depth, feat = features.shape
    rows //= 2
    groups = 2 if slots % 2 == 0 else 1
    feature_parts = 4 if tiles % 4 == 0 else 1
    height = slots // groups * rows
    out = (peers, slots * feat // LANES + int(with_ids), rows // peers, LANES)
    return pl.pallas_call(
        functools.partial(product_kernel, with_ids, groups, feature_parts),
        in_specs=[spec(pltpu.SMEM)] + [spec(pltpu.HBM)] * 4,
        out_specs=spec(pltpu.VMEM),
        out_shape=jax.ShapeDtypeStruct(out, F32),
        scratch_shapes=[
            pltpu.VMEM((slots, rows, width), F32),
            pltpu.VMEM((slots // groups, tiles, rows, depth), F32),
            pltpu.VMEM((2, 2 * height, tiles * depth), BF16),
            pltpu.VMEM((tiles * depth, feat), BF16),
            pltpu.VMEM((tiles * depth, feat), BF16),
            pltpu.VMEM(features.shape, F32),
            pltpu.SMEM(row_ids.shape, I32),
            pltpu.SMEM(col_ids.shape, I32),
            pltpu.SemaphoreType.DMA((slots,)),
            pltpu.SemaphoreType.DMA((feature_parts,)),
            pltpu.SemaphoreType.DMA((2,)),
        ],
        compiler_params=params(PRODUCT_VMEM_BYTES),
        cost_estimate=pl.CostEstimate(
            flops=6 * slots * rows * tiles * depth * feat,
            bytes_accessed=4 * (slots * rows * width + tiles * depth * feat),
            transcendentals=0,
        ),
        name="product",
    )(part, blocks, row_ids, col_ids, features)


def add_by_row(row_of, pieces_ref, tables, slots):
    peers = pieces_ref.shape[0]
    tiles = tables[0].shape[1]

    def add_peer(peer, carry):
        for slot in range(slots):
            row = row_of(peer, slot)
            table = tables[slot % len(tables)]
            table[row] = table[row] + pieces_ref[peer, slot * tiles : (slot + 1) * tiles]
        return carry

    lax.fori_loop(0, peers, add_peer, 0, unroll=UNROLL)


def sum_kernel(slots, pieces_ref, out_ref, ids_out, other, ids, sem):
    ids_out[...] = pieces_ref[:, pieces_ref.shape[1] - 1].astype(I32)
    ids_copy = pltpu.make_async_copy(ids_out, ids, sem)
    ids_copy.start()
    out_ref[...] = jnp.zeros_like(out_ref)
    other[...] = jnp.zeros_like(other)
    ids_copy.wait()

    add_by_row(lambda peer, slot: ids[peer, 0, slot], pieces_ref, (out_ref, other), slots)
    out_ref[...] += other[...]


def sum_pieces(pieces, row_blocks, slots):
    peers, places, rows, _ = pieces.shape
    tiles = (places - 1) // slots
    return pl.pallas_call(
        functools.partial(sum_kernel, slots),
        in_specs=[spec(pltpu.VMEM)],
        out_specs=(spec(pltpu.VMEM), spec(pltpu.VMEM)),
        out_shape=(
            jax.ShapeDtypeStruct((row_blocks, tiles, rows, LANES), F32),
            jax.ShapeDtypeStruct((peers, rows, LANES), I32),
        ),
        scratch_shapes=[
            pltpu.VMEM((row_blocks, tiles, rows, LANES), F32),
            pltpu.SMEM((peers, rows, LANES), I32),
            pltpu.SemaphoreType.DMA,
        ],
        compiler_params=params(),
        name="sum_pieces",
    )(pieces)


def update_kernel(slots, ids_ref, pieces_ref, got_ref, factor_ref, out_ref, total, other, left):
    row_blocks, tiles, rows, _ = out_ref.shape
    total[...] = got_ref[...]
    other[...] = jnp.zeros_like(other)
    add_by_row(
        lambda peer, slot: ids_ref[peer * slots + slot], pieces_ref, (total, other), slots
    )
    for row in range(row_blocks):
        for t in range(tiles):
            here = slice(row * rows, (row + 1) * rows), slice(t * LANES, (t + 1) * LANES)
            left[here] = total[row, t] + other[row, t]
    out = dot3(*split(jnp.tanh(left[...])), *split(factor_ref[...]))
    for row in range(row_blocks):
        for t in range(tiles):
            out_ref[row, t] = out[row * rows : (row + 1) * rows, t * LANES : (t + 1) * LANES]


def update(ids, pieces, got, factor, slots):
    row_blocks, tiles, rows, _ = got.shape
    return pl.pallas_call(
        functools.partial(update_kernel, slots),
        in_specs=[spec(pltpu.SMEM), spec(pltpu.VMEM), spec(pltpu.VMEM), spec(pltpu.VMEM)],
        out_specs=spec(pltpu.VMEM),
        out_shape=jax.ShapeDtypeStruct(got.shape, F32),
        scratch_shapes=[
            pltpu.VMEM(got.shape, F32),
            pltpu.VMEM(got.shape, F32),
            pltpu.VMEM((row_blocks * rows, tiles * LANES), F32),
        ],
        compiler_params=params(),
        name="update",
    )(ids, pieces, got, factor)


def answer_kernel(slots, ids_ref, half_ref, table_ref, out_ref):
    peers = out_ref.shape[0]
    tiles = table_ref.shape[1]
    chips = peers // 2
    first = half_ref[0] * peers

    def pick(chip, carry):
        for core in range(2):
            peer = core * chips + chip
            for slot in range(slots):
                row = ids_ref[peer * slots + slot]
                out_ref[peer, slot * tiles : (slot + 1) * tiles] = table_ref[row]
            out_ref[peer, slots * tiles :] = table_ref[first + chip * 2 + core]
        return carry

    lax.fori_loop(0, chips, pick, 0, unroll=UNROLL)


def answer(ids, half, table, peers, slots, flops):
    _, tiles, rows, _ = table.shape
    out = (peers, (slots + 1) * tiles, rows, LANES)
    return pl.pallas_call(
        functools.partial(answer_kernel, slots),
        in_specs=[spec(pltpu.SMEM), spec(pltpu.SMEM), spec(pltpu.VMEM)],
        out_specs=spec(pltpu.VMEM),
        out_shape=jax.ShapeDtypeStruct(out, F32),
        compiler_params=params(),
        cost_estimate=pl.CostEstimate(
            flops=flops, bytes_accessed=8 * peers * out[1] * rows * LANES, transcendentals=0
        ),
        name="answer",
    )(ids, half, table)


def place_kernel(slots, part_ref, answers_ref, *refs):
    owned_hbm, returned_hbm, whole, sems = refs[-4:]
    peers, places, rows, _ = answers_ref.shape
    chips = peers // 2
    tiles = places // (slots + 1)
    at = pl.ds(part_ref[0] * chips, chips)
    copies = []
    for place in range(slots + 1):
        cut = slice(place * tiles, (place + 1) * tiles)
        for core in range(2):
            whole[place, :, :, core * rows : (core + 1) * rows] = answers_ref[
                core * chips : (core + 1) * chips, cut
            ]
        target = returned_hbm.at[place, at] if place < slots else owned_hbm.at[at]
        copies.append(pltpu.make_async_copy(whole.at[place], target, sems.at[place]))
        copies[-1].start()
    for copy in copies:
        copy.wait()


def place(part, answers, slots, earlier=()):
    peers, places, rows, _ = answers.shape
    chips = peers // 2
    tiles = places // (slots + 1)
    owned = (2 * chips, tiles, 2 * rows, LANES)
    return pl.pallas_call(
        functools.partial(place_kernel, slots),
        in_specs=[spec(pltpu.SMEM), spec(pltpu.VMEM)] + [spec(pltpu.HBM)] * len(earlier),
        out_specs=(spec(pltpu.HBM), spec(pltpu.HBM)),
        out_shape=(
            jax.ShapeDtypeStruct(owned, F32),
            jax.ShapeDtypeStruct((slots, *owned), F32),
        ),
        scratch_shapes=[
            pltpu.VMEM((slots + 1, chips, tiles, 2 * rows, LANES), F32),
            pltpu.SemaphoreType.DMA((slots + 1,)),
        ],
        input_output_aliases={2 + i: i for i in range(len(earlier))},
        compiler_params=params(),
        name="place",
    )(part, answers, *earlier)


def local(blocks, features, col_ids, row_ids, factor):
    slots = blocks.shape[0]
    peer_axes = ("core", "chip")
    peers = lax.axis_size(peer_axes)
    row_blocks = peers * lax.axis_size("half")
    here = lax.axis_index("half").astype(I32).reshape(1)
    there = 1 - here
    swap = [(0, 1), (1, 0)]
    here, there, row_ids = lax.optimization_barrier((here, there, row_ids))

    far = product(blocks, features, col_ids, row_ids, there, peers, True)
    far = lax.all_to_all(far, peer_axes, 0, 0)
    near = product(blocks, features, col_ids, row_ids, here, peers, False)
    near = lax.all_to_all(near, peer_axes, 0, 0)
    far_sums, ids = sum_pieces(far, row_blocks, slots)
    got = lax.ppermute(far_sums, "half", swap)
    ids = ids[:, 0, :slots].reshape(-1)
    near_rows = update(ids, near, got, factor, slots)

    far_rows = lax.ppermute(near_rows, "half", swap)
    near_answers = lax.all_to_all(answer(ids, here, near_rows, peers, slots, 0), peer_axes, 0, 0)
    far_answers = answer(ids, here, far_rows, peers, slots, 1 << 34)
    far_answers = lax.all_to_all(far_answers, peer_axes, 0, 0)
    outputs = place(here, near_answers, slots)
    owned_rows, returned = place(there, far_answers, slots, outputs)
    feat = returned.shape[2] * LANES
    owned_rows = owned_rows.transpose(0, 2, 1, 3).reshape(-1, feat)
    returned = returned.transpose(0, 1, 3, 2, 4).reshape(-1, feat)
    return owned_rows, returned


def solution(mesh):
    devices = mesh.devices.reshape(2, mesh.devices.size // 4, 2)
    axes = ("half", "chip", "core")
    split_mesh = Mesh(devices, axes)
    return jax.shard_map(
        local,
        mesh=split_mesh,
        in_specs=(P(axes, None, None), P(axes, None, None), P(axes, None), P(axes), P()),
        out_specs=(P(axes, None), P(axes, None)),
        check_vma=False,
    )
```

```python
import functools

import jax
import jax.numpy as jnp
from jax import lax
from jax.experimental import pallas as pl
from jax.experimental.pallas import tpu as pltpu
from jax.sharding import Mesh
from jax.sharding import PartitionSpec as P

F32 = jnp.float32
BF16 = jnp.bfloat16
I32 = jnp.int32
LANES = 128
UNROLL = 8
VMEM_BYTES = 24 << 20
PRODUCT_VMEM_BYTES = 60 << 20


def split(value):
    high = value.astype(BF16)
    return high, (value - high.astype(F32)).astype(BF16)


def dot3(a_high, a_low, b_high, b_low):
    dot = functools.partial(jnp.dot, preferred_element_type=F32)
    return dot(a_high, b_high) + dot(a_high, b_low) + dot(a_low, b_high)


def spec(space):
    return pl.BlockSpec(memory_space=space)


def params(vmem_bytes=VMEM_BYTES):
    return pltpu.CompilerParams(vmem_limit_bytes=vmem_bytes)


def product_kernel(
    with_ids, groups, feature_parts, part_ref, blocks_hbm, ids_hbm, cols_hbm, features_hbm, out_ref,
    blocks, total, left, f_high, f_low, features, ids, cols, block_sems, feature_sems, id_sems,
):
    slots, per_row = cols.shape
    tiles, depth, feat = features.shape
    rows = blocks.shape[1]
    peers, _, piece_rows, _ = out_ref.shape
    in_group = slots // groups
    height = in_group * rows
    part_tiles = tiles // feature_parts
    first = pl.multiple_of(part_ref[0] * rows, rows)
    block_copies = [
        pltpu.make_async_copy(
            blocks_hbm.at[k, pl.ds(first, rows)], blocks.at[k], block_sems.at[k]
        )
        for k in range(slots)
    ]
    feature_copies = [
        pltpu.make_async_copy(
            features_hbm.at[pl.ds(k * part_tiles, part_tiles)],
            features.at[pl.ds(k * part_tiles, part_tiles)],
            feature_sems.at[k],
        )
        for k in range(feature_parts)
    ]
    id_copies = [
        pltpu.make_async_copy(cols_hbm, cols, id_sems.at[0]),
        pltpu.make_async_copy(ids_hbm, ids, id_sems.at[1]),
    ]
    for copy in id_copies + block_copies[:in_group] + feature_copies + block_copies[in_group:]:
        copy.start()
    for copy in id_copies:
        copy.wait()

    def combine(group):
        for s in range(in_group):
            slot = group * in_group + s
            block_copies[slot].wait()
            total[s] = jnp.zeros_like(total[s])
            for j in range(per_row):
                tile = cols[slot, j]
                total[s, tile] = total[s, tile] + blocks[slot, :, j * depth : (j + 1) * depth]
            for tile in range(tiles):
                high, low = split(total[s, tile])
                cut = slice(tile * depth, (tile + 1) * depth)
                left[group % 2, s * rows : (s + 1) * rows, cut] = high
                left[group % 2, height + s * rows : height + (s + 1) * rows, cut] = low

    def multiply(group):
        width = min(feat, 2 * LANES)
        dot = functools.partial(jnp.dot, preferred_element_type=F32)
        for n in range(0, feat, width):
            cut = slice(n, n + width)
            both = dot(left[group % 2], f_high[:, cut])
            both = both[:height] + both[height:] + dot(left[group % 2, :height], f_low[:, cut])
            for s in range(in_group):
                for t in range(0, width, LANES):
                    piece = both[s * rows : (s + 1) * rows, t : t + LANES]
                    place = ((group * in_group + s) * feat + n + t) // LANES
                    piece = piece.reshape(peers // 2, 2, piece_rows, LANES)
                    out_ref[: peers // 2, place] = piece[:, 0]
                    out_ref[peers // 2 :, place] = piece[:, 1]

    def split_tile(tile, carry):
        high, low = split(features[tile])
        here = pl.ds(pl.multiple_of(tile * depth, depth), depth)
        f_high[here, :] = high
        f_low[here, :] = low
        return carry

    combine(0)
    for k in range(feature_parts):
        feature_copies[k].wait()
        lax.fori_loop(k * part_tiles, (k + 1) * part_tiles, split_tile, 0)
    for group in range(groups):
        if group + 1 < groups:
            combine(group + 1)
        multiply(group)
    if with_ids:
        lane = lax.broadcasted_iota(I32, (peers, piece_rows, LANES), 2)
        shown = jnp.zeros((peers, piece_rows, LANES), I32)
        for slot in range(slots):
            shown = jnp.where(lane == slot, ids[slot], shown)
        out_ref[:, slots * feat // LANES] = shown.astype(F32)


def product(blocks, features, col_ids, row_ids, part, peers, with_ids):
    slots, rows, width = blocks.shape
    tiles, depth, feat = features.shape
    rows //= 2
    groups = 2 if slots % 2 == 0 else 1
    feature_parts = 4 if tiles % 4 == 0 else 1
    height = slots // groups * rows
    out = (peers, slots * feat // LANES + int(with_ids), rows // peers, LANES)
    return pl.pallas_call(
        functools.partial(product_kernel, with_ids, groups, feature_parts),
        in_specs=[spec(pltpu.SMEM)] + [spec(pltpu.HBM)] * 4,
        out_specs=spec(pltpu.VMEM),
        out_shape=jax.ShapeDtypeStruct(out, F32),
        scratch_shapes=[
            pltpu.VMEM((slots, rows, width), F32),
            pltpu.VMEM((slots // groups, tiles, rows, depth), F32),
            pltpu.VMEM((2, 2 * height, tiles * depth), BF16),
            pltpu.VMEM((tiles * depth, feat), BF16),
            pltpu.VMEM((tiles * depth, feat), BF16),
            pltpu.VMEM(features.shape, F32),
            pltpu.SMEM(row_ids.shape, I32),
            pltpu.SMEM(col_ids.shape, I32),
            pltpu.SemaphoreType.DMA((slots,)),
            pltpu.SemaphoreType.DMA((feature_parts,)),
            pltpu.SemaphoreType.DMA((2,)),
        ],
        compiler_params=params(PRODUCT_VMEM_BYTES),
        cost_estimate=pl.CostEstimate(
            flops=6 * slots * rows * tiles * depth * feat,
            bytes_accessed=4 * (slots * rows * width + tiles * depth * feat),
            transcendentals=0,
        ),
        name="product",
    )(part, blocks, row_ids, col_ids, features)


def add_by_row(row_of, pieces_ref, tables, slots):
    peers = pieces_ref.shape[0]
    tiles = tables[0].shape[1]

    def add_peer(peer, carry):
        for slot in range(slots):
            row = row_of(peer, slot)
            table = tables[slot % len(tables)]
            table[row] = table[row] + pieces_ref[peer, slot * tiles : (slot + 1) * tiles]
        return carry

    lax.fori_loop(0, peers, add_peer, 0, unroll=UNROLL)


def sum_kernel(slots, pieces_ref, out_ref, ids_out, other, ids, sem):
    ids_out[...] = pieces_ref[:, pieces_ref.shape[1] - 1].astype(I32)
    ids_copy = pltpu.make_async_copy(ids_out, ids, sem)
    ids_copy.start()
    out_ref[...] = jnp.zeros_like(out_ref)
    other[...] = jnp.zeros_like(other)
    ids_copy.wait()

    add_by_row(lambda peer, slot: ids[peer, 0, slot], pieces_ref, (out_ref, other), slots)
    out_ref[...] += other[...]


def sum_pieces(pieces, row_blocks, slots):
    peers, places, rows, _ = pieces.shape
    tiles = (places - 1) // slots
    return pl.pallas_call(
        functools.partial(sum_kernel, slots),
        in_specs=[spec(pltpu.VMEM)],
        out_specs=(spec(pltpu.VMEM), spec(pltpu.VMEM)),
        out_shape=(
            jax.ShapeDtypeStruct((row_blocks, tiles, rows, LANES), F32),
            jax.ShapeDtypeStruct((peers, rows, LANES), I32),
        ),
        scratch_shapes=[
            pltpu.VMEM((row_blocks, tiles, rows, LANES), F32),
            pltpu.SMEM((peers, rows, LANES), I32),
            pltpu.SemaphoreType.DMA,
        ],
        compiler_params=params(),
        name="sum_pieces",
    )(pieces)


def update_kernel(
    slots, ids_ref, half_ref, pieces_ref, got_ref, factor_ref, out_ref, answers_ref, total, other, left
):
    row_blocks, tiles, rows, _ = out_ref.shape
    total[...] = got_ref[...]
    other[...] = jnp.zeros_like(other)
    add_by_row(
        lambda peer, slot: ids_ref[peer * slots + slot], pieces_ref, (total, other), slots
    )
    for row in range(row_blocks):
        for t in range(tiles):
            here = slice(row * rows, (row + 1) * rows), slice(t * LANES, (t + 1) * LANES)
            left[here] = total[row, t] + other[row, t]
    out = dot3(*split(jnp.tanh(left[...])), *split(factor_ref[...]))
    for row in range(row_blocks):
        for t in range(tiles):
            out_ref[row, t] = out[row * rows : (row + 1) * rows, t * LANES : (t + 1) * LANES]
    answer_kernel(slots, ids_ref, half_ref, out_ref, answers_ref)


def update(ids, half, pieces, got, factor, slots):
    row_blocks, tiles, rows, _ = got.shape
    answers = (pieces.shape[0], (slots + 1) * tiles, rows, LANES)
    return pl.pallas_call(
        functools.partial(update_kernel, slots),
        in_specs=[spec(pltpu.SMEM)] * 2 + [spec(pltpu.VMEM)] * 3,
        out_specs=(spec(pltpu.VMEM), spec(pltpu.VMEM)),
        out_shape=(
            jax.ShapeDtypeStruct(got.shape, F32),
            jax.ShapeDtypeStruct(answers, F32),
        ),
        scratch_shapes=[
            pltpu.VMEM(got.shape, F32),
            pltpu.VMEM(got.shape, F32),
            pltpu.VMEM((row_blocks * rows, tiles * LANES), F32),
        ],
        compiler_params=params(),
        name="update",
    )(ids, half, pieces, got, factor)


def answer_kernel(slots, ids_ref, half_ref, table_ref, out_ref):
    peers = out_ref.shape[0]
    tiles = table_ref.shape[1]
    chips = peers // 2
    first = half_ref[0] * peers

    def pick(chip, carry):
        for core in range(2):
            peer = core * chips + chip
            for slot in range(slots):
                row = ids_ref[peer * slots + slot]
                out_ref[peer, slot * tiles : (slot + 1) * tiles] = table_ref[row]
            out_ref[peer, slots * tiles :] = table_ref[first + chip * 2 + core]
        return carry

    lax.fori_loop(0, chips, pick, 0, unroll=UNROLL)


def answer(ids, half, table, peers, slots, flops):
    _, tiles, rows, _ = table.shape
    out = (peers, (slots + 1) * tiles, rows, LANES)
    return pl.pallas_call(
        functools.partial(answer_kernel, slots),
        in_specs=[spec(pltpu.SMEM), spec(pltpu.SMEM), spec(pltpu.VMEM)],
        out_specs=spec(pltpu.VMEM),
        out_shape=jax.ShapeDtypeStruct(out, F32),
        compiler_params=params(),
        cost_estimate=pl.CostEstimate(
            flops=flops, bytes_accessed=8 * peers * out[1] * rows * LANES, transcendentals=0
        ),
        name="answer",
    )(ids, half, table)


def place_kernel(slots, part_ref, answers_ref, *refs):
    owned_hbm, returned_hbm, whole, sems = refs[-4:]
    peers, places, rows, _ = answers_ref.shape
    chips = peers // 2
    tiles = places // (slots + 1)
    at = pl.ds(part_ref[0] * chips, chips)
    copies = []
    for place in range(slots + 1):
        cut = slice(place * tiles, (place + 1) * tiles)
        for core in range(2):
            whole[place, :, :, core * rows : (core + 1) * rows] = answers_ref[
                core * chips : (core + 1) * chips, cut
            ]
        target = returned_hbm.at[place, at] if place < slots else owned_hbm.at[at]
        copies.append(pltpu.make_async_copy(whole.at[place], target, sems.at[place]))
        copies[-1].start()
    for copy in copies:
        copy.wait()


def place(part, answers, slots, earlier=()):
    peers, places, rows, _ = answers.shape
    chips = peers // 2
    tiles = places // (slots + 1)
    owned = (2 * chips, tiles, 2 * rows, LANES)
    return pl.pallas_call(
        functools.partial(place_kernel, slots),
        in_specs=[spec(pltpu.SMEM), spec(pltpu.VMEM)] + [spec(pltpu.HBM)] * len(earlier),
        out_specs=(spec(pltpu.HBM), spec(pltpu.HBM)),
        out_shape=(
            jax.ShapeDtypeStruct(owned, F32),
            jax.ShapeDtypeStruct((slots, *owned), F32),
        ),
        scratch_shapes=[
            pltpu.VMEM((slots + 1, chips, tiles, 2 * rows, LANES), F32),
            pltpu.SemaphoreType.DMA((slots + 1,)),
        ],
        input_output_aliases={2 + i: i for i in range(len(earlier))},
        compiler_params=params(),
        name="place",
    )(part, answers, *earlier)


def local(blocks, features, col_ids, row_ids, factor):
    slots = blocks.shape[0]
    peer_axes = ("core", "chip")
    peers = lax.axis_size(peer_axes)
    row_blocks = peers * lax.axis_size("half")
    here = lax.axis_index("half").astype(I32).reshape(1)
    there = 1 - here
    swap = [(0, 1), (1, 0)]
    here, there, row_ids = lax.optimization_barrier((here, there, row_ids))

    far = product(blocks, features, col_ids, row_ids, there, peers, True)
    far = lax.all_to_all(far, peer_axes, 0, 0)
    near = product(blocks, features, col_ids, row_ids, here, peers, False)
    near = lax.all_to_all(near, peer_axes, 0, 0)
    far_sums, ids = sum_pieces(far, row_blocks, slots)
    got = lax.ppermute(far_sums, "half", swap)
    ids = ids[:, 0, :slots].reshape(-1)
    near_rows, near_answers = update(ids, here, near, got, factor, slots)

    far_rows = lax.ppermute(near_rows, "half", swap)
    near_answers = lax.all_to_all(near_answers, peer_axes, 0, 0)
    far_answers = answer(ids, here, far_rows, peers, slots, 1 << 34)
    far_answers = lax.all_to_all(far_answers, peer_axes, 0, 0)
    outputs = place(here, near_answers, slots)
    owned_rows, returned = place(there, far_answers, slots, outputs)
    feat = returned.shape[2] * LANES
    owned_rows = owned_rows.transpose(0, 2, 1, 3).reshape(-1, feat)
    returned = returned.transpose(0, 1, 3, 2, 4).reshape(-1, feat)
    return owned_rows, returned


def solution(mesh):
    devices = mesh.devices.reshape(2, mesh.devices.size // 4, 2)
    axes = ("half", "chip", "core")
    split_mesh = Mesh(devices, axes)
    return jax.shard_map(
        local,
        mesh=split_mesh,
        in_specs=(P(axes, None, None), P(axes, None, None), P(axes, None), P(axes), P()),
        out_specs=(P(axes, None), P(axes, None)),
        check_vma=False,
    )
```

```python
import functools

import jax
import jax.numpy as jnp
from jax import lax
from jax.experimental import pallas as pl
from jax.experimental.pallas import tpu as pltpu
from jax.sharding import Mesh
from jax.sharding import PartitionSpec as P

F32 = jnp.float32
BF16 = jnp.bfloat16
I32 = jnp.int32
LANES = 128
UNROLL = 8
VMEM_BYTES = 24 << 20
PRODUCT_VMEM_BYTES = 60 << 20


def split(value):
    high = value.astype(BF16)
    return high, (value - high.astype(F32)).astype(BF16)


def dot3(a_high, a_low, b_high, b_low):
    dot = functools.partial(jnp.dot, preferred_element_type=F32)
    return dot(a_high, b_high) + dot(a_high, b_low) + dot(a_low, b_high)


def spec(space):
    return pl.BlockSpec(memory_space=space)


def params(vmem_bytes=VMEM_BYTES):
    return pltpu.CompilerParams(vmem_limit_bytes=vmem_bytes)


def product_kernel(
    with_ids, groups, feature_parts, part_ref, blocks_hbm, ids_hbm, cols_hbm, features_hbm, out_ref,
    blocks, total, left, f_high, f_low, features, ids, cols, block_sems, feature_sems, id_sems,
):
    slots, per_row = cols.shape
    tiles, depth, feat = features.shape
    rows = blocks.shape[1]
    peers, _, piece_rows, _ = out_ref.shape
    in_group = slots // groups
    height = in_group * rows
    part_tiles = tiles // feature_parts
    first = pl.multiple_of(part_ref[0] * rows, rows)
    block_copies = [
        pltpu.make_async_copy(
            blocks_hbm.at[k, pl.ds(first, rows)], blocks.at[k], block_sems.at[k]
        )
        for k in range(slots)
    ]
    feature_copies = [
        pltpu.make_async_copy(
            features_hbm.at[pl.ds(k * part_tiles, part_tiles)],
            features.at[pl.ds(k * part_tiles, part_tiles)],
            feature_sems.at[k],
        )
        for k in range(feature_parts)
    ]
    id_copies = [
        pltpu.make_async_copy(cols_hbm, cols, id_sems.at[0]),
        pltpu.make_async_copy(ids_hbm, ids, id_sems.at[1]),
    ]
    for copy in id_copies + feature_copies + block_copies:
        copy.start()
    for copy in id_copies:
        copy.wait()

    def combine(group):
        for s in range(in_group):
            slot = group * in_group + s
            block_copies[slot].wait()
            total[s] = jnp.zeros_like(total[s])
            for j in range(per_row):
                tile = cols[slot, j]
                total[s, tile] = total[s, tile] + blocks[slot, :, j * depth : (j + 1) * depth]
            for tile in range(tiles):
                high, low = split(total[s, tile])
                cut = slice(tile * depth, (tile + 1) * depth)
                left[group % 2, s * rows : (s + 1) * rows, cut] = high
                left[group % 2, height + s * rows : height + (s + 1) * rows, cut] = low

    def multiply(group):
        width = min(feat, 2 * LANES)
        dot = functools.partial(jnp.dot, preferred_element_type=F32)
        for n in range(0, feat, width):
            cut = slice(n, n + width)
            both = dot(left[group % 2], f_high[:, cut])
            both = both[:height] + both[height:] + dot(left[group % 2, :height], f_low[:, cut])
            for s in range(in_group):
                for t in range(0, width, LANES):
                    piece = both[s * rows : (s + 1) * rows, t : t + LANES]
                    place = ((group * in_group + s) * feat + n + t) // LANES
                    piece = piece.reshape(peers // 2, 2, piece_rows, LANES)
                    out_ref[: peers // 2, place] = piece[:, 0]
                    out_ref[peers // 2 :, place] = piece[:, 1]

    def split_tile(tile, carry):
        high, low = split(features[tile])
        here = pl.ds(pl.multiple_of(tile * depth, depth), depth)
        f_high[here, :] = high
        f_low[here, :] = low
        return carry

    for k in range(feature_parts):
        feature_copies[k].wait()
        lax.fori_loop(k * part_tiles, (k + 1) * part_tiles, split_tile, 0)
    combine(0)
    for group in range(groups):
        if group + 1 < groups:
            combine(group + 1)
        multiply(group)
    if with_ids:
        lane = lax.broadcasted_iota(I32, (peers, piece_rows, LANES), 2)
        shown = jnp.zeros((peers, piece_rows, LANES), I32)
        for slot in range(slots):
            shown = jnp.where(lane == slot, ids[slot], shown)
        out_ref[:, slots * feat // LANES] = shown.astype(F32)


def product(blocks, features, col_ids, row_ids, part, peers, with_ids):
    slots, rows, width = blocks.shape
    tiles, depth, feat = features.shape
    rows //= 2
    groups = 2 if slots % 2 == 0 else 1
    feature_parts = 4 if tiles % 4 == 0 else 1
    height = slots // groups * rows
    out = (peers, slots * feat // LANES + int(with_ids), rows // peers, LANES)
    return pl.pallas_call(
        functools.partial(product_kernel, with_ids, groups, feature_parts),
        in_specs=[spec(pltpu.SMEM)] + [spec(pltpu.HBM)] * 4,
        out_specs=spec(pltpu.VMEM),
        out_shape=jax.ShapeDtypeStruct(out, F32),
        scratch_shapes=[
            pltpu.VMEM((slots, rows, width), F32),
            pltpu.VMEM((slots // groups, tiles, rows, depth), F32),
            pltpu.VMEM((2, 2 * height, tiles * depth), BF16),
            pltpu.VMEM((tiles * depth, feat), BF16),
            pltpu.VMEM((tiles * depth, feat), BF16),
            pltpu.VMEM(features.shape, F32),
            pltpu.SMEM(row_ids.shape, I32),
            pltpu.SMEM(col_ids.shape, I32),
            pltpu.SemaphoreType.DMA((slots,)),
            pltpu.SemaphoreType.DMA((feature_parts,)),
            pltpu.SemaphoreType.DMA((2,)),
        ],
        compiler_params=params(PRODUCT_VMEM_BYTES),
        cost_estimate=pl.CostEstimate(
            flops=6 * slots * rows * tiles * depth * feat,
            bytes_accessed=4 * (slots * rows * width + tiles * depth * feat),
            transcendentals=0,
        ),
        name="product",
    )(part, blocks, row_ids, col_ids, features)


def add_by_row(row_of, pieces_ref, tables, slots):
    peers = pieces_ref.shape[0]
    tiles = tables[0].shape[1]

    def add_peer(peer, carry):
        for slot in range(slots):
            row = row_of(peer, slot)
            table = tables[slot % len(tables)]
            table[row] = table[row] + pieces_ref[peer, slot * tiles : (slot + 1) * tiles]
        return carry

    lax.fori_loop(0, peers, add_peer, 0, unroll=UNROLL)


def sum_kernel(slots, pieces_ref, out_ref, ids_out, other, ids, sem):
    ids_out[...] = pieces_ref[:, pieces_ref.shape[1] - 1].astype(I32)
    ids_copy = pltpu.make_async_copy(ids_out, ids, sem)
    ids_copy.start()
    out_ref[...] = jnp.zeros_like(out_ref)
    other[...] = jnp.zeros_like(other)
    ids_copy.wait()

    add_by_row(lambda peer, slot: ids[peer, 0, slot], pieces_ref, (out_ref, other), slots)
    out_ref[...] += other[...]


def sum_pieces(pieces, row_blocks, slots):
    peers, places, rows, _ = pieces.shape
    tiles = (places - 1) // slots
    return pl.pallas_call(
        functools.partial(sum_kernel, slots),
        in_specs=[spec(pltpu.VMEM)],
        out_specs=(spec(pltpu.VMEM), spec(pltpu.VMEM)),
        out_shape=(
            jax.ShapeDtypeStruct((row_blocks, tiles, rows, LANES), F32),
            jax.ShapeDtypeStruct((peers, rows, LANES), I32),
        ),
        scratch_shapes=[
            pltpu.VMEM((row_blocks, tiles, rows, LANES), F32),
            pltpu.SMEM((peers, rows, LANES), I32),
            pltpu.SemaphoreType.DMA,
        ],
        compiler_params=params(),
        name="sum_pieces",
    )(pieces)


def update_kernel(
    slots, ids_ref, half_ref, pieces_ref, got_ref, factor_ref, out_ref, answers_ref, total, other, left
):
    row_blocks, tiles, rows, _ = out_ref.shape
    total[...] = got_ref[...]
    other[...] = jnp.zeros_like(other)
    add_by_row(
        lambda peer, slot: ids_ref[peer * slots + slot], pieces_ref, (total, other), slots
    )
    for row in range(row_blocks):
        for t in range(tiles):
            here = slice(row * rows, (row + 1) * rows), slice(t * LANES, (t + 1) * LANES)
            left[here] = total[row, t] + other[row, t]
    out = dot3(*split(jnp.tanh(left[...])), *split(factor_ref[...]))
    for row in range(row_blocks):
        for t in range(tiles):
            out_ref[row, t] = out[row * rows : (row + 1) * rows, t * LANES : (t + 1) * LANES]
    answer_kernel(slots, ids_ref, half_ref, out_ref, answers_ref)


def update(ids, half, pieces, got, factor, slots):
    row_blocks, tiles, rows, _ = got.shape
    answers = (pieces.shape[0], (slots + 1) * tiles, rows, LANES)
    return pl.pallas_call(
        functools.partial(update_kernel, slots),
        in_specs=[spec(pltpu.SMEM)] * 2 + [spec(pltpu.VMEM)] * 3,
        out_specs=(spec(pltpu.VMEM), spec(pltpu.VMEM)),
        out_shape=(
            jax.ShapeDtypeStruct(got.shape, F32),
            jax.ShapeDtypeStruct(answers, F32),
        ),
        scratch_shapes=[
            pltpu.VMEM(got.shape, F32),
            pltpu.VMEM(got.shape, F32),
            pltpu.VMEM((row_blocks * rows, tiles * LANES), F32),
        ],
        compiler_params=params(),
        name="update",
    )(ids, half, pieces, got, factor)


def answer_kernel(slots, ids_ref, half_ref, table_ref, out_ref):
    peers = out_ref.shape[0]
    tiles = table_ref.shape[1]
    chips = peers // 2
    first = half_ref[0] * peers

    def pick(chip, carry):
        for core in range(2):
            peer = core * chips + chip
            for slot in range(slots):
                row = ids_ref[peer * slots + slot]
                out_ref[peer, slot * tiles : (slot + 1) * tiles] = table_ref[row]
            out_ref[peer, slots * tiles :] = table_ref[first + chip * 2 + core]
        return carry

    lax.fori_loop(0, chips, pick, 0, unroll=UNROLL)


def answer(ids, half, table, peers, slots, flops):
    _, tiles, rows, _ = table.shape
    out = (peers, (slots + 1) * tiles, rows, LANES)
    return pl.pallas_call(
        functools.partial(answer_kernel, slots),
        in_specs=[spec(pltpu.SMEM), spec(pltpu.SMEM), spec(pltpu.VMEM)],
        out_specs=spec(pltpu.VMEM),
        out_shape=jax.ShapeDtypeStruct(out, F32),
        compiler_params=params(),
        cost_estimate=pl.CostEstimate(
            flops=flops, bytes_accessed=8 * peers * out[1] * rows * LANES, transcendentals=0
        ),
        name="answer",
    )(ids, half, table)


def place_kernel(slots, part_ref, answers_ref, *refs):
    owned_hbm, returned_hbm, whole, sems = refs[-4:]
    peers, places, rows, _ = answers_ref.shape
    chips = peers // 2
    tiles = places // (slots + 1)
    at = pl.ds(part_ref[0] * chips, chips)
    copies = []
    for place in range(slots + 1):
        cut = slice(place * tiles, (place + 1) * tiles)
        for core in range(2):
            whole[place, :, :, core * rows : (core + 1) * rows] = answers_ref[
                core * chips : (core + 1) * chips, cut
            ]
        target = returned_hbm.at[place, at] if place < slots else owned_hbm.at[at]
        copies.append(pltpu.make_async_copy(whole.at[place], target, sems.at[place]))
        copies[-1].start()
    for copy in copies:
        copy.wait()


def place(part, answers, slots, earlier=()):
    peers, places, rows, _ = answers.shape
    chips = peers // 2
    tiles = places // (slots + 1)
    owned = (2 * chips, tiles, 2 * rows, LANES)
    return pl.pallas_call(
        functools.partial(place_kernel, slots),
        in_specs=[spec(pltpu.SMEM), spec(pltpu.VMEM)] + [spec(pltpu.HBM)] * len(earlier),
        out_specs=(spec(pltpu.HBM), spec(pltpu.HBM)),
        out_shape=(
            jax.ShapeDtypeStruct(owned, F32),
            jax.ShapeDtypeStruct((slots, *owned), F32),
        ),
        scratch_shapes=[
            pltpu.VMEM((slots + 1, chips, tiles, 2 * rows, LANES), F32),
            pltpu.SemaphoreType.DMA((slots + 1,)),
        ],
        input_output_aliases={2 + i: i for i in range(len(earlier))},
        compiler_params=params(),
        name="place",
    )(part, answers, *earlier)


def local(blocks, features, col_ids, row_ids, factor):
    slots = blocks.shape[0]
    peer_axes = ("core", "chip")
    peers = lax.axis_size(peer_axes)
    row_blocks = peers * lax.axis_size("half")
    here = lax.axis_index("half").astype(I32).reshape(1)
    there = 1 - here
    swap = [(0, 1), (1, 0)]
    here, there, row_ids = lax.optimization_barrier((here, there, row_ids))

    far = product(blocks, features, col_ids, row_ids, there, peers, True)
    far = lax.all_to_all(far, peer_axes, 0, 0)
    near = product(blocks, features, col_ids, row_ids, here, peers, False)
    near = lax.all_to_all(near, peer_axes, 0, 0)
    far_sums, ids = sum_pieces(far, row_blocks, slots)
    got = lax.ppermute(far_sums, "half", swap)
    ids = ids[:, 0, :slots].reshape(-1)
    near_rows, near_answers = update(ids, here, near, got, factor, slots)

    far_rows = lax.ppermute(near_rows, "half", swap)
    near_answers = lax.all_to_all(near_answers, peer_axes, 0, 0)
    far_answers = answer(ids, here, far_rows, peers, slots, 1 << 34)
    far_answers = lax.all_to_all(far_answers, peer_axes, 0, 0)
    outputs = place(here, near_answers, slots)
    owned_rows, returned = place(there, far_answers, slots, outputs)
    feat = returned.shape[2] * LANES
    owned_rows = owned_rows.transpose(0, 2, 1, 3).reshape(-1, feat)
    returned = returned.transpose(0, 1, 3, 2, 4).reshape(-1, feat)
    return owned_rows, returned


def solution(mesh):
    devices = mesh.devices.reshape(2, mesh.devices.size // 4, 2)
    axes = ("half", "chip", "core")
    split_mesh = Mesh(devices, axes)
    return jax.shard_map(
        local,
        mesh=split_mesh,
        in_specs=(P(axes, None, None), P(axes, None, None), P(axes, None), P(axes), P()),
        out_specs=(P(axes, None), P(axes, None)),
        check_vma=False,
    )
```
